256 devices in a mesh: ens: 4 (over y_hi, core), grid: 64 (over x, y_lo, z).
Axes of the slice: x: 4, y: 4 (y_hi: 2, y_lo: 2; y = y_hi * 2 + y_lo), z: 8, core: 2. Of those that a mesh axis runs over, the one named last changes fastest.
Arguments:
- members: bfloat16 [8, 16384, 1024], P('ens', 'grid'), may hold values from -6 to 6
- observed_truth: float32 [16384, 100], P('grid'), may hold values from -6 to 6
- cell_measure: float32 [16384], P('grid'), may hold values from 0.25 to 12, as said below
- reach: int32 [16384], P('grid'), may hold values from 1 to 128, as said below
- w_query: bfloat16 [1024, 1024], replicated, may hold values from -0.1875 to 0.1875
- w_key: bfloat16 [1024, 1024], replicated, may hold values from -0.1875 to 0.1875
- w_value: bfloat16 [1024, 1024], replicated, may hold values from -0.1875 to 0.1875
- w_out: bfloat16 [1024, 1024], replicated, may hold values from -0.75 to 0.75
- readout_coefficients: bfloat16 [1024, 100], replicated, may hold values from -0.1875 to 0.1875
Outputs:
- loss: float32 [], replicated
- adjoint_members: bfloat16 [8, 16384, 1024], P('ens', 'grid')
The draws below stay inside these ranges and needn't reach their ends.
Inputs may be any that keep to these rules, and one draw needn't show every extreme that they name: Each point's window reach lies between 1 and 128; in every block of 256 points some have reach 128. `cell_measure`: positive point weights.
All inputs are finite; a program needn't handle non-finite values.
Results may differ from the reference program's by a relative error of at most 0.02.
Values may be sent and summed in bfloat16 or wider, within the bound.
A program may use at most 128 MiB of HBM per device.

```python
import jax
import jax.numpy as jnp
from jax import lax

D = 1024
VARS = 100
HEADS = 16
P_SIZE = 256
HALF = 128
MEMBERS = 8
NPOINTS = 16384


def draw_reach(key, part):
    key = jax.random.fold_in(key, 11)
    drawn = jax.random.randint(key, (NPOINTS,), max(1, HALF // 2), HALF + 1, dtype=jnp.int32)
    position = jnp.arange(NPOINTS, dtype=jnp.int32)
    return jnp.where(position % 4 == 0, HALF, drawn).astype(jnp.int32)


def draw_cell_measure(key, part):
    key = jax.random.fold_in(key, 23)
    position = jnp.arange(NPOINTS, dtype=jnp.float32) / NPOINTS
    rough = jnp.exp(jax.random.uniform(key, (NPOINTS,), jnp.float32, -1.0, 1.0))
    return (rough * (1.0 + 2.0 * position)).astype(jnp.float32)


def steps_of(stream_key, dims, cuts, least, top_value):
    factor_of = 1.0
    for dim, shards_of in cuts:
        draws = jax.random.uniform(jax.random.fold_in(jax.random.fold_in(stream_key, 6), dim), (shards_of,), jnp.float32, least / len(cuts), top_value / len(cuts))
        factor_of = factor_of * jnp.repeat(jnp.exp(draws), dims[dim] // shards_of).reshape((-1,) + (1,) * (len(dims) - 1 - dim))
    return factor_of


def noise(rng, dims, width, most, shards=(), kind=jnp.bfloat16):
    values = jax.random.normal(rng, dims, jnp.float32) * width
    if len(shards) > 0:
        values = steps_of(rng, dims, shards, -0.22, 0.18) * values
    return jnp.clip(values, min=-most, max=most).astype(kind)


def setup_inputs(seed: int = 0) -> dict:
    splits = jax.random.split(jax.random.key(seed), 10)
    members = noise(splits[0], (MEMBERS, NPOINTS, D), 1.0, 6.0, ((0, 4), (1, 64)))
    observed_truth = noise(splits[1], (NPOINTS, VARS), 1.0, 6.0, ((0, 64),), jnp.float32)
    cell_measure = draw_cell_measure(jax.random.fold_in(splits[9], 71), 0)
    reach = draw_reach(jax.random.fold_in(splits[9], 71), 0)
    w_query = noise(splits[4], (D, D), D ** -0.5, 0.1875)
    w_key = noise(splits[5], (D, D), D ** -0.5, 0.1875)
    w_value = noise(splits[6], (D, D), D ** -0.5, 0.1875)
    w_out = noise(splits[7], (D, D), (D // 16) ** -0.5, 0.75)
    readout_coefficients = noise(splits[8], (D, VARS), D ** -0.5, 0.1875)
    return dict(members=members, observed_truth=observed_truth, cell_measure=cell_measure, reach=reach, w_query=w_query, w_key=w_key, w_value=w_value, w_out=w_out, readout_coefficients=readout_coefficients)


eps = 1e-05
kernel_soft = 0.1

def widened_copy(block):
    return lax.optimization_barrier(block).astype(jnp.float32)

def layer_stats(block):
    values = block.astype(jnp.float32)
    centred = values - lax.optimization_barrier(jnp.mean(values, axis=-1, keepdims=True))
    inverse = lax.rsqrt(lax.optimization_barrier(jnp.mean(centred * centred, axis=-1, keepdims=True)) + eps)
    return (centred * inverse, inverse)

def norm_back(adjoint, normed, inverse):
    return inverse * (adjoint - lax.optimization_barrier(jnp.mean(adjoint, axis=-1, keepdims=True)) - normed * lax.optimization_barrier(jnp.mean(adjoint * normed, axis=-1, keepdims=True)))

def line_inner_results(left, weight):
    flat = left.reshape(-1, left.shape[-1])
    return jnp.dot(flat, weight, preferred_element_type=jnp.float32).reshape(left.shape[:-1] + (weight.shape[1],))

def line_inner_derivative(left, weight):
    flat = left.reshape(-1, left.shape[-1])
    return jnp.dot(flat, weight.T, preferred_element_type=jnp.float32).reshape(left.shape[:-1] + (weight.shape[0],))

def window_mask(first_query, first_key, key_count, reach, total):
    query_pos = first_query + jnp.arange(reach.shape[0], dtype=jnp.int32)
    key_pos = first_key + jnp.arange(key_count, dtype=jnp.int32)
    distance = jnp.abs(key_pos[None, :] - query_pos[:, None])
    inside = (key_pos >= 0) & (key_pos < total)
    return (distance <= reach[:, None]) & inside[None, :]

def split_heads(block):
    return block.astype(jnp.float32).reshape(block.shape[0], HEADS, block.shape[1] // HEADS)

def probabilities(query, keys, mask):
    depth = query.shape[1] // HEADS
    scores = jnp.einsum('qhd,khd->hqk', split_heads(query), split_heads(keys)) * depth ** (-0.5)
    scores = jnp.where(mask[None], scores, -1e+30)
    top = lax.optimization_barrier(jnp.max(scores, axis=-1, keepdims=True))
    weights = jnp.exp(scores - top) * mask[None].astype(jnp.float32)
    return weights / lax.optimization_barrier(jnp.sum(weights, axis=-1, keepdims=True))

def attend(query, keys, values, mask):
    weights = widened_copy(probabilities(query, keys, mask).astype(jnp.bfloat16))
    blended_hidden = jnp.einsum('hqk,khd->qhd', weights, split_heads(values))
    return blended_hidden.reshape(query.shape).astype(jnp.bfloat16)

def attend_back(query, keys, values, mask, adjoint_out):
    depth = query.shape[1] // HEADS
    attention = probabilities(query, keys, mask)
    weights = widened_copy(attention.astype(jnp.bfloat16))
    adjoint_heads = split_heads(adjoint_out)
    adjoint_prob = jnp.einsum('qhd,khd->hqk', adjoint_heads, split_heads(values))
    value_terms = jnp.einsum('hqk,qhd->khd', weights, adjoint_heads).reshape(keys.shape)
    adjoint_score = attention * (adjoint_prob - lax.optimization_barrier(jnp.sum(attention * adjoint_prob, axis=-1, keepdims=True))) * depth ** (-0.5)
    adjoint_score = widened_copy(adjoint_score.astype(jnp.bfloat16))
    adjoint_query = jnp.einsum('hqk,khd->qhd', adjoint_score, split_heads(keys)).reshape(query.shape).astype(jnp.bfloat16)
    key_terms = jnp.einsum('hqk,qhd->khd', adjoint_score, split_heads(query)).reshape(keys.shape)
    return (adjoint_query, key_terms, value_terms)

def penalty_by_realization(prediction_entries, observed_truth, cell_measure):
    overall_tally = prediction_entries.shape[0]
    diagonal_dispersion = prediction_entries - observed_truth[None]
    own_kernel = jnp.sqrt(diagonal_dispersion * diagonal_dispersion + kernel_soft * kernel_soft)
    realization_dispersion = prediction_entries[:, None] - prediction_entries[None]
    similarity_table = jnp.sqrt(realization_dispersion * realization_dispersion + kernel_soft * kernel_soft)
    pair_sum = lax.optimization_barrier(jnp.sum(similarity_table, axis=1)) - kernel_soft
    pair_slope = lax.optimization_barrier(jnp.sum(realization_dispersion / similarity_table, axis=1))
    factor = 1.0 / (overall_tally - 1)
    part = jnp.sum(cell_measure[:, None] * lax.optimization_barrier(jnp.sum(own_kernel - 0.5 * factor * pair_sum, axis=0)))
    adjoint = cell_measure[None, :, None] * (diagonal_dispersion / own_kernel - factor * pair_slope)
    return (part, adjoint.astype(jnp.bfloat16))

def rim_project(key_rim, value_rim, w_key, w_value):
    key_b = key_rim.astype(jnp.bfloat16)
    value_b = value_rim.astype(jnp.bfloat16)
    term = line_inner_derivative(key_b, w_key) + line_inner_derivative(value_b, w_value)
    return widened_copy(term.astype(jnp.bfloat16))

def reference(members, observed_truth, cell_measure, reach, w_query, w_key, w_value, w_out, readout_coefficients):
    span = P_SIZE + 2 * HALF
    padded = jnp.pad(members, ((0, 0), (HALF, HALF), (0, 0)))
    blocks = NPOINTS // P_SIZE

    def first_pass(index):
        start = index * P_SIZE
        widened = lax.dynamic_slice_in_dim(padded, start, span, 1)
        normed_wide, inverse_wide = layer_stats(widened)
        normed_b = normed_wide.astype(jnp.bfloat16)
        query = line_inner_results(normed_b[:, HALF:HALF + P_SIZE], w_query).astype(jnp.bfloat16)
        keys = line_inner_results(normed_b, w_key).astype(jnp.bfloat16)
        values = line_inner_results(normed_b, w_value).astype(jnp.bfloat16)
        reach_block = lax.dynamic_slice_in_dim(reach, start, P_SIZE, 0)
        observed_truth_tile = lax.dynamic_slice_in_dim(observed_truth, start, P_SIZE, 0)
        cell_measure_tile = lax.dynamic_slice_in_dim(cell_measure, start, P_SIZE, 0)
        mask = window_mask(start, start - HALF, span, reach_block, NPOINTS)
        attended = lax.map(lambda item: attend(item[0], item[1], item[2], mask), (query, keys, values))
        blended_hidden = widened[:, HALF:HALF + P_SIZE].astype(jnp.float32) + line_inner_results(attended, w_out)
        prediction_entries = line_inner_results(blended_hidden.astype(jnp.bfloat16), readout_coefficients)
        part, prediction_derivative = penalty_by_realization(prediction_entries, observed_truth_tile, cell_measure_tile)
        blended_derivative = line_inner_derivative(prediction_derivative, readout_coefficients)
        adjoint_attended = line_inner_derivative(blended_derivative.astype(jnp.bfloat16), w_out).astype(jnp.bfloat16)
        adjoint_query, key_terms, value_terms = lax.map(lambda item: attend_back(item[0], item[1], item[2], mask, item[3]), (query, keys, values, adjoint_attended))
        partial_sum = blended_derivative + norm_back(line_inner_derivative(adjoint_query, w_query), normed_wide[:, HALF:HALF + P_SIZE], inverse_wide[:, HALF:HALF + P_SIZE])
        return (part, partial_sum, key_terms, value_terms)
    parts, partials, key_blocks, value_blocks = lax.map(first_pass, jnp.arange(blocks, dtype=jnp.int32))

    def second_pass(index):
        block = lax.dynamic_slice_in_dim(members, index * P_SIZE, P_SIZE, 1)
        normed, inverse = layer_stats(block)
        key_own = key_blocks[index][:, HALF:HALF + P_SIZE].astype(jnp.bfloat16)
        value_own = value_blocks[index][:, HALF:HALF + P_SIZE].astype(jnp.bfloat16)
        adjoint_normed = line_inner_derivative(key_own, w_key) + line_inner_derivative(value_own, w_value)
        after = jnp.minimum(index + 1, blocks - 1)
        before = jnp.maximum(index - 1, 0)
        has_after = (index + 1 < blocks).astype(jnp.float32)
        has_before = (index > 0).astype(jnp.float32)
        from_above = rim_project(key_blocks[after][:, :HALF], value_blocks[after][:, :HALF], w_key, w_value) * has_after
        from_below = rim_project(key_blocks[before][:, HALF + P_SIZE:], value_blocks[before][:, HALF + P_SIZE:], w_key, w_value) * has_before
        rim_normed = jnp.zeros(adjoint_normed.shape, jnp.float32)
        rim_normed = rim_normed.at[:, P_SIZE - HALF:].add(from_above)
        rim_normed = rim_normed.at[:, :HALF].add(from_below)
        adjoint_normed = adjoint_normed + rim_normed
        return (partials[index] + norm_back(adjoint_normed, normed, inverse)).astype(jnp.bfloat16)
    adjoint_blocks = lax.map(second_pass, jnp.arange(blocks, dtype=jnp.int32))
    adjoint_members = jnp.transpose(adjoint_blocks, (1, 0, 2, 3)).reshape(MEMBERS, NPOINTS, D)
    loss = jnp.sum(parts) / (MEMBERS * NPOINTS * VARS)
    return (loss, adjoint_members)
```

```python
import functools
import math

import jax
import jax.numpy as jnp
from jax import lax
from jax.experimental import pallas as pl
from jax.experimental.pallas import tpu as pltpu
from jax.sharding import PartitionSpec as P

MESH = pl.DeviceIdType.MESH
F32 = jnp.float32
BF16 = jnp.bfloat16
HEAD = 64
HALF = 128
LANES = 128
COLS = 256
WINDOW = 3 * HALF
EPS = 1e-05
SOFT2 = 0.01
SOFT = 0.1
LOG2E = math.log2(math.e)
LN2 = math.log(2.0)

NN = (((1,), (0,)), ((), ()))
NT = (((1,), (1,)), ((), ()))


def dot(a, b, dims=NN):
    return lax.dot_general(a, b, dims, preferred_element_type=F32)


def flip(index, bit):
    return index + bit * (1 - 2 * ((index // bit) % 2))


def normalise(block):
    values = block.astype(F32)
    centred = values - jnp.mean(values, axis=-1, keepdims=True)
    inverse = lax.rsqrt(jnp.mean(centred * centred, axis=-1, keepdims=True) + EPS)
    return centred * inverse, inverse


def per_head(pair):
    low = lax.broadcasted_iota(jnp.int32, pair.shape, 1) < HEAD
    zero = jnp.zeros_like(pair)
    return jnp.concatenate([jnp.where(low, pair, zero), jnp.where(low, zero, pair)], axis=0)


def own_head(wide):
    both = jnp.concatenate([wide[:HEAD, :HALF], wide[HEAD:, HALF:]], axis=0)
    return both.T


def kernel(
    ens_size,
    grid_size,
    nvars,
    members,
    truth_in,
    measure_in,
    reach_in,
    w_query,
    w_key,
    w_value,
    w_out,
    readout_in,
    loss_out,
    out,
    mem,
    halo,
    wq,
    wk,
    wv,
    wo,
    readout,
    truth,
    measure,
    bias,
    normed_own,
    normed_halo,
    q_s,
    k_s,
    v_s,
    p_s,
    attended,
    forecasts,
    adj_mixed,
    adj_mixed_b,
    adj_attended,
    dq_s,
    dk_s,
    dv_s,
    rim_k,
    rim_v,
    rim_out,
    rim_in,
    adj_normed,
    loss_acc,
    loss_in,
    load_sem,
    halo_send,
    halo_recv,
    ens_send,
    ens_recv,
    rim_send,
    rim_recv,
    loss_send,
    loss_recv,
):
    count, rows, width = members.shape
    pairs = width // LANES
    chunks = width // COLS
    tiles = rows // HALF
    ens = lax.axis_index("ens")
    grid = lax.axis_index("grid")
    right = lax.rem(grid + 1, grid_size)
    left = lax.rem(grid + grid_size - 1, grid_size)
    first = grid * rows
    total_points = rows * grid_size
    ens_partners = [{"ens": flip(ens, 1)}, {"ens": flip(ens, 2)}, {"ens": flip(flip(ens, 1), 2)}]
    ens_partners = ens_partners[: ens_size - 1]
    rounds = [{"ens": flip(ens, 1 << b)} for b in range(ens_size.bit_length() - 1)]
    rounds += [{"grid": flip(grid, 1 << b)} for b in range(grid_size.bit_length() - 1)]

    def remote(source, target, send, recv, device):
        return pltpu.make_async_remote_copy(
            src_ref=source,
            dst_ref=target,
            send_sem=send,
            recv_sem=recv,
            device_id=device,
            device_id_type=MESH,
        )

    loads = []
    for m in range(count):
        loads.append(pltpu.make_async_copy(members.at[m], mem.at[m], load_sem.at[m]))
    for n, (source, target) in enumerate(((w_query, wq), (w_key, wk), (w_value, wv), (w_out, wo))):
        loads.append(pltpu.make_async_copy(source, target, load_sem.at[count + n]))
    for load in loads:
        load.start()

    barrier = pltpu.get_barrier_semaphore()
    greeted = [{"grid": left}, {"grid": right}] + ens_partners + rounds
    for device in greeted:
        pl.semaphore_signal(barrier, inc=1, device_id=device, device_id_type=MESH)
    pl.semaphore_wait(barrier, len(greeted))

    halo_copies = []
    for m in range(count):
        to_left = remote(
            members.at[m, pl.ds(0, HALF)],
            halo.at[m, pl.ds(HALF, HALF)],
            halo_send.at[m, 0],
            halo_recv.at[m, 0],
            {"grid": left},
        )
        to_right = remote(
            members.at[m, pl.ds(rows - HALF, HALF)],
            halo.at[m, pl.ds(0, HALF)],
            halo_send.at[m, 1],
            halo_recv.at[m, 1],
            {"grid": right},
        )
        to_left.start()
        to_right.start()
        halo_copies.append((to_left, to_right))

    readout[...] = jnp.zeros_like(readout)
    readout[:, :nvars] = readout_in[...]
    truth[...] = jnp.zeros_like(truth)
    truth[:, :nvars] = truth_in[...]
    for t in range(tiles):
        part = pl.ds(t * HALF, HALF)
        row = jnp.broadcast_to(measure_in[:, t * HALF : (t + 1) * HALF], (HALF, HALF))
        measure[part, :] = row.T
        offset = lax.broadcasted_iota(jnp.int32, (WINDOW, HALF), 0) - HALF
        query = lax.broadcasted_iota(jnp.int32, (WINDOW, HALF), 1)
        point = offset + (first + t * HALF)
        reach = reach_in[:, t * HALF : (t + 1) * HALF]
        inside = (jnp.abs(offset - query) <= reach) & (point >= 0) & (point < total_points)
        bias[t] = jnp.where(inside, 0.0, -1e30).astype(F32)

    for m in range(count):
        loads[m].wait()
        for t in range(tiles):
            normed, _ = normalise(mem[m, t * HALF : (t + 1) * HALF])
            normed_own[pl.ds(m * rows + t * HALF, HALF), :] = normed.astype(BF16)
    for n in range(4):
        loads[count + n].wait()

    def project_own(c, carry):
        columns = pl.ds(pl.multiple_of(c * COLS, COLS), COLS)
        left_side = normed_own[...]
        query = (dot(left_side, wq[:, columns]) * (HEAD**-0.5 * LOG2E)).astype(BF16)
        for m in range(count):
            for j in range(2):
                q_s[m, 2 * c + j] = query[m * rows : (m + 1) * rows, j * LANES : (j + 1) * LANES]
        for weight, target in ((wk, k_s), (wv, v_s)):
            result = dot(left_side, weight[:, columns]).astype(BF16)
            for m in range(count):
                for j in range(2):
                    target[m, 2 * c + j, pl.ds(HALF, rows), :] = result[
                        m * rows : (m + 1) * rows, j * LANES : (j + 1) * LANES
                    ]
        return carry

    lax.fori_loop(0, chunks, project_own, 0)

    def attend(m, p, carry):
        keys = k_s[m, p]
        values_t = v_s[m, p].T
        for t in range(tiles):
            query = per_head(q_s[m, p, t * HALF : (t + 1) * HALF])
            window = slice(t * HALF, t * HALF + WINDOW)
            scores = dot(keys[window], query, NT)
            scores = scores + jnp.concatenate([bias[t]] * 2, axis=1)
            top = jnp.max(scores, axis=0, keepdims=True)
            weights = jnp.exp2(scores - top)
            weights = weights * (1.0 / jnp.sum(weights, axis=0, keepdims=True))
            weights = weights.astype(BF16)
            p_s[m, t, p] = weights
            blended = own_head(dot(values_t[:, window], weights))
            attended[
                pl.ds(m * rows + t * HALF, HALF), pl.ds(pl.multiple_of(p * LANES, LANES), LANES)
            ] = blended.astype(BF16)
        return carry

    ens_copies = []
    for m in range(count):
        for copy in halo_copies[m]:
            copy.wait()
        for t in range(2):
            part = pl.ds(t * HALF, HALF)
            normed, _ = normalise(halo[m, part])
            normed_halo[part, :] = normed.astype(BF16)

        def project_halo(c, carry, m=m):
            columns = pl.ds(pl.multiple_of(c * COLS, COLS), COLS)
            for weight, target in ((wk, k_s), (wv, v_s)):
                result = dot(normed_halo[...], weight[:, columns]).astype(BF16)
                for j in range(2):
                    lanes = slice(j * LANES, (j + 1) * LANES)
                    target[m, 2 * c + j, pl.ds(0, HALF), :] = result[:HALF, lanes]
                    target[m, 2 * c + j, pl.ds(HALF + rows, HALF), :] = result[HALF:, lanes]
            return carry

        lax.fori_loop(0, chunks, project_halo, 0)
        lax.fori_loop(0, pairs, functools.partial(attend, m), 0)

        def mix(c, total, m=m):
            columns = pl.ds(pl.multiple_of(c * COLS, COLS), COLS)
            mixed = dot(attended[pl.ds(m * rows, rows), :], wo[:, columns])
            mixed = mixed + mem[m, :, columns].astype(F32)
            return total + dot(mixed.astype(BF16), readout[columns, :])

        forecasts[0, m] = lax.fori_loop(0, chunks, mix, jnp.zeros((rows, LANES), F32))
        for slot, device in enumerate(ens_partners):
            copy = remote(
                forecasts.at[0, m],
                forecasts.at[slot + 1, m],
                ens_send.at[slot, m],
                ens_recv.at[slot, m],
                device,
            )
            copy.start()
            ens_copies.append(copy)

    for copy in ens_copies:
        copy.wait()

    realizations = count * ens_size
    factor = 1.0 / (realizations - 1)
    real = lax.broadcasted_iota(jnp.int32, (HALF, LANES), 1) < nvars
    score = jnp.zeros((HALF, LANES), F32)
    for t in range(tiles):
        part = slice(t * HALF, (t + 1) * HALF)
        weight = measure[part, :]
        for m in range(count):
            mine = forecasts[0, m, part]
            pair_sum = jnp.zeros((HALF, LANES), F32)
            pair_slope = jnp.zeros((HALF, LANES), F32)
            for slot in range(ens_size):
                for other in range(count):
                    if slot == 0 and other == m:
                        continue
                    gap = mine - forecasts[slot, other, part]
                    square = gap * gap + SOFT2
                    root = lax.rsqrt(square)
                    pair_sum = pair_sum + square * root
                    pair_slope = pair_slope + gap * root
            gap = mine - truth[part, :]
            square = gap * gap + SOFT2
            root = lax.rsqrt(square)
            score = score + weight * (square * root - 0.5 * factor * pair_sum)
            slope = weight * (gap * root - factor * pair_slope)
            adj_mixed_b[pl.ds(m * rows + t * HALF, HALF), pl.ds(0, LANES)] = slope.astype(BF16)
    score = jnp.where(real, score, 0.0)
    loss_acc[0] = jnp.broadcast_to(jnp.sum(score, keepdims=True), (8, LANES))

    pending = []

    def loss_step(stage):
        if stage > 0 and stage <= len(rounds):
            pending[stage - 1].wait()
            loss_acc[stage] = loss_acc[stage - 1] + loss_in[stage - 1]
        if stage < len(rounds):
            copy = remote(
                loss_acc.at[stage],
                loss_in.at[stage],
                loss_send.at[stage],
                loss_recv.at[stage],
                rounds[stage],
            )
            copy.start()
            pending.append(copy)

    loss_step(0)

    slopes = adj_mixed_b[:, :LANES]

    def spread(c, carry):
        columns = pl.ds(pl.multiple_of(c * COLS, COLS), COLS)
        adj_mixed[:, columns] = dot(slopes, readout[columns, :], NT)
        return carry

    lax.fori_loop(0, chunks, spread, 0)
    adj_mixed_b[...] = adj_mixed[...].astype(BF16)

    def back_out(c, carry):
        columns = pl.ds(pl.multiple_of(c * COLS, COLS), COLS)
        adj_attended[:, columns] = dot(adj_mixed_b[...], wo[columns, :], NT).astype(BF16)
        return carry

    lax.fori_loop(0, chunks, back_out, 0)
    loss_step(1)

    def attend_back(m, p, carry):
        keys = k_s[m, p]
        keys_t = keys.T
        values = v_s[m, p]
        lanes = pl.ds(pl.multiple_of(p * LANES, LANES), LANES)
        key_terms = []
        value_terms = []
        for t in range(tiles):
            mine = pl.ds(m * rows + t * HALF, HALF)
            window = slice(t * HALF, t * HALF + WINDOW)
            query = per_head(q_s[m, p, t * HALF : (t + 1) * HALF])
            adjoint = per_head(adj_attended[mine, lanes])
            weights = p_s[m, t, p]
            wide = weights.astype(F32)
            adj_prob = dot(values[window], adjoint, NT)
            shift = jnp.sum(wide * adj_prob, axis=0, keepdims=True)
            adj_score = (wide * (adj_prob - shift)).astype(BF16)
            adj_query = own_head(dot(keys_t[:, window], adj_score)) * HEAD**-0.5
            dq_s[mine, lanes] = adj_query.astype(BF16)
            key_terms.append(dot(adj_score, query) * LN2)
            value_terms.append(dot(weights, adjoint))
        for terms, own, rim in ((key_terms, dk_s, rim_k), (value_terms, dv_s, rim_v)):
            low, high = terms
            rim[pl.ds(0, HALF), lanes] = low[:HALF].astype(BF16)
            rim[pl.ds(HALF, HALF), lanes] = high[2 * HALF :].astype(BF16)
            own[pl.ds(m * rows, rows), lanes] = (low[HALF:] + high[: 2 * HALF]).astype(BF16)
        return carry

    rim_copies = []
    for m in range(count):
        lax.fori_loop(0, pairs // 2, functools.partial(attend_back, m), 0)
        loss_step(2 + 3 * m)
        lax.fori_loop(pairs // 2, pairs, functools.partial(attend_back, m), 0)
        loss_step(3 + 3 * m)

        def project_rim(c, carry, m=m):
            columns = pl.ds(pl.multiple_of(c * COLS, COLS), COLS)
            term = dot(rim_k[...], wk[columns, :], NT) + dot(rim_v[...], wv[columns, :], NT)
            rim_out[m, :, columns] = term.astype(BF16)
            return carry

        lax.fori_loop(0, chunks, project_rim, 0)
        to_left = remote(
            rim_out.at[m, pl.ds(0, HALF)],
            rim_in.at[m, pl.ds(HALF, HALF)],
            rim_send.at[m, 0],
            rim_recv.at[m, 0],
            {"grid": left},
        )
        to_right = remote(
            rim_out.at[m, pl.ds(HALF, HALF)],
            rim_in.at[m, pl.ds(0, HALF)],
            rim_send.at[m, 1],
            rim_recv.at[m, 1],
            {"grid": right},
        )
        to_left.start()
        to_right.start()
        rim_copies.append((to_left, to_right))
        loss_step(4 + 3 * m)

    def back_own(c, carry):
        columns = pl.ds(pl.multiple_of(c * COLS, COLS), COLS)
        adj_normed[:, columns] = (
            dot(dq_s[...], wq[columns, :], NT)
            + dot(dk_s[...], wk[columns, :], NT)
            + dot(dv_s[...], wv[columns, :], NT)
        )
        return carry

    lax.fori_loop(0, chunks, back_own, 0)
    for stage in range(8, len(rounds) + 1):
        loss_step(stage)
    loss_out[...] = loss_acc[len(rounds), 0:1, 0:1] * (1.0 / (realizations * total_points * nvars))

    for m in range(count):
        for copy in rim_copies[m]:
            copy.wait()
        for t in range(tiles):
            part = slice(t * HALF, (t + 1) * HALF)
            mine = pl.ds(m * rows + t * HALF, HALF)
            normed, inverse = normalise(mem[m, part])
            adjoint = adj_normed[mine, :] + rim_in[m, part].astype(F32)
            adjoint = inverse * (
                adjoint
                - jnp.mean(adjoint, axis=-1, keepdims=True)
                - normed * jnp.mean(adjoint * normed, axis=-1, keepdims=True)
            )
            out[m, part] = (adj_mixed[mine, :] + adjoint).astype(BF16)


def per_device(
    ens_size,
    grid_size,
    members,
    observed_truth,
    cell_measure,
    reach,
    w_query,
    w_key,
    w_value,
    w_out,
    readout_coefficients,
):
    count, rows, width = members.shape
    nvars = observed_truth.shape[1]
    pairs = width // LANES
    tiles = rows // HALF
    all_rows = count * rows
    stages = ens_size.bit_length() + grid_size.bit_length() - 2
    vmem = pl.BlockSpec(memory_space=pltpu.VMEM)
    anywhere = pl.BlockSpec(memory_space=pl.ANY)
    dma = pltpu.SemaphoreType.DMA
    loss, adjoint = pl.pallas_call(
        functools.partial(kernel, ens_size, grid_size, nvars),
        out_shape=(
            jax.ShapeDtypeStruct((1, 1), F32),
            jax.ShapeDtypeStruct(members.shape, BF16),
        ),
        in_specs=[anywhere, vmem, vmem, vmem, anywhere, anywhere, anywhere, anywhere, vmem],
        out_specs=(vmem, vmem),
        scratch_shapes=[
            pltpu.VMEM((count, rows, width), BF16),
            pltpu.VMEM((count, 2 * HALF, width), BF16),
            pltpu.VMEM((width, width), BF16),
            pltpu.VMEM((width, width), BF16),
            pltpu.VMEM((width, width), BF16),
            pltpu.VMEM((width, width), BF16),
            pltpu.VMEM((width, LANES), BF16),
            pltpu.VMEM((rows, LANES), F32),
            pltpu.VMEM((rows, LANES), F32),
            pltpu.VMEM((tiles, WINDOW, HALF), F32),
            pltpu.VMEM((all_rows, width), BF16),
            pltpu.VMEM((2 * HALF, width), BF16),
            pltpu.VMEM((count, pairs, rows, LANES), BF16),
            pltpu.VMEM((count, pairs, rows + 2 * HALF, LANES), BF16),
            pltpu.VMEM((count, pairs, rows + 2 * HALF, LANES), BF16),
            pltpu.VMEM((count, tiles, pairs, WINDOW, 2 * HALF), BF16),
            pltpu.VMEM((all_rows, width), BF16),
            pltpu.VMEM((ens_size, count, rows, LANES), F32),
            pltpu.VMEM((all_rows, width), F32),
            pltpu.VMEM((all_rows, width), BF16),
            pltpu.VMEM((all_rows, width), BF16),
            pltpu.VMEM((all_rows, width), BF16),
            pltpu.VMEM((all_rows, width), BF16),
            pltpu.VMEM((all_rows, width), BF16),
            pltpu.VMEM((2 * HALF, width), BF16),
            pltpu.VMEM((2 * HALF, width), BF16),
            pltpu.VMEM((count, 2 * HALF, width), BF16),
            pltpu.VMEM((count, 2 * HALF, width), BF16),
            pltpu.VMEM((all_rows, width), F32),
            pltpu.VMEM((stages + 1, 8, LANES), F32),
            pltpu.VMEM((stages, 8, LANES), F32),
            dma((count + 4,)),
            dma((count, 2)),
            dma((count, 2)),
            dma((ens_size - 1, count)),
            dma((ens_size - 1, count)),
            dma((count, 2)),
            dma((count, 2)),
            dma((stages,)),
            dma((stages,)),
        ],
        compiler_params=pltpu.CompilerParams(
            collective_id=0, has_side_effects=True, vmem_limit_bytes=60 * 1024 * 1024
        ),
        cost_estimate=pl.CostEstimate(
            flops=15_000_000_000, bytes_accessed=12_000_000, transcendentals=4_000_000
        ),
    )(
        members,
        observed_truth,
        cell_measure.reshape(1, rows),
        reach.reshape(1, rows),
        w_query,
        w_key,
        w_value,
        w_out,
        readout_coefficients,
    )
    return loss[0, 0], adjoint


def solution(mesh):
    return jax.shard_map(
        functools.partial(per_device, mesh.shape["ens"], mesh.shape["grid"]),
        mesh=mesh,
        in_specs=(
            P("ens", "grid", None),
            P("grid", None),
            P("grid"),
            P("grid"),
            P(),
            P(),
            P(),
            P(),
            P(),
        ),
        out_specs=(P(), P("ens", "grid", None)),
        check_vma=False,
    )
```

```python
import functools
import math

import jax
import jax.numpy as jnp
from jax import lax
from jax.experimental import pallas as pl
from jax.experimental.pallas import tpu as pltpu
from jax.sharding import PartitionSpec as P

MESH = pl.DeviceIdType.MESH
F32 = jnp.float32
BF16 = jnp.bfloat16
HEAD = 64
HALF = 128
LANES = 128
COLS = 256
WINDOW = 3 * HALF
EPS = 1e-05
SOFT2 = 0.01
SOFT = 0.1
LOG2E = math.log2(math.e)
LN2 = math.log(2.0)

NN = (((1,), (0,)), ((), ()))
NT = (((1,), (1,)), ((), ()))


def dot(a, b, dims=NN):
    return lax.dot_general(a, b, dims, preferred_element_type=F32)


def flip(index, bit):
    return index + bit * (1 - 2 * ((index // bit) % 2))


def normalise(block):
    values = block.astype(F32)
    centred = values - jnp.mean(values, axis=-1, keepdims=True)
    inverse = lax.rsqrt(jnp.mean(centred * centred, axis=-1, keepdims=True) + EPS)
    return centred * inverse, inverse


def per_head(pair):
    low = lax.broadcasted_iota(jnp.int32, pair.shape, 1) < HEAD
    zero = jnp.zeros_like(pair)
    return jnp.concatenate([jnp.where(low, pair, zero), jnp.where(low, zero, pair)], axis=0)


def own_lanes(tall):
    low = lax.broadcasted_iota(jnp.int32, (HALF, LANES), 1) < HEAD
    return jnp.where(low, tall[:HALF], tall[HALF:])


def own_head(wide):
    both = jnp.concatenate([wide[:HEAD, :HALF], wide[HEAD:, HALF:]], axis=0)
    return both.T


def kernel(
    ens_size,
    grid_size,
    nvars,
    members,
    truth_in,
    measure_in,
    reach_in,
    w_query,
    w_key,
    w_value,
    w_out,
    readout_in,
    loss_out,
    out,
    mem,
    halo,
    wq,
    wk,
    wv,
    wo,
    readout,
    truth_t,
    truth,
    measure,
    bias,
    normed_own,
    normed_halo,
    q_s,
    k_s,
    v_s,
    p_s,
    attended,
    forecasts,
    shared,
    adj_mixed,
    adj_mixed_b,
    adj_attended,
    dq_s,
    dk_s,
    dv_s,
    rim_k,
    rim_v,
    rim_out,
    rim_in,
    adj_normed,
    loss_acc,
    loss_in,
    load_sem,
    halo_send,
    halo_recv,
    ens_send,
    ens_recv,
    rim_send,
    rim_recv,
    loss_send,
    loss_recv,
):
    count, rows, width = members.shape
    pairs = width // LANES
    chunks = width // COLS
    tiles = rows // HALF
    ens = lax.axis_index("ens")
    grid = lax.axis_index("grid")
    right = lax.rem(grid + 1, grid_size)
    left = lax.rem(grid + grid_size - 1, grid_size)
    first = grid * rows
    total_points = rows * grid_size
    ens_partners = [{"ens": flip(ens, 1)}, {"ens": flip(ens, 2)}, {"ens": flip(flip(ens, 1), 2)}]
    ens_partners = ens_partners[: ens_size - 1]
    rounds = [{"ens": flip(ens, 1 << b)} for b in range(ens_size.bit_length() - 1)]
    rounds += [{"grid": flip(grid, 1 << b)} for b in range(grid_size.bit_length() - 1)]

    def remote(source, target, send, recv, device):
        return pltpu.make_async_remote_copy(
            src_ref=source,
            dst_ref=target,
            send_sem=send,
            recv_sem=recv,
            device_id=device,
            device_id_type=MESH,
        )

    loads = []
    for m in range(count):
        loads.append(pltpu.make_async_copy(members.at[m], mem.at[m], load_sem.at[m]))
    for n, (source, target) in enumerate(((w_query, wq), (w_key, wk), (w_value, wv), (w_out, wo))):
        loads.append(pltpu.make_async_copy(source, target, load_sem.at[count + n]))
    for load in loads:
        load.start()

    barrier = pltpu.get_barrier_semaphore()
    greeted = [{"grid": left}, {"grid": right}] + ens_partners + rounds
    for device in greeted:
        pl.semaphore_signal(barrier, inc=1, device_id=device, device_id_type=MESH)
    pl.semaphore_wait(barrier, len(greeted))

    halo_copies = []
    for m in range(count):
        to_left = remote(
            members.at[m, pl.ds(0, HALF)],
            halo.at[m, pl.ds(HALF, HALF)],
            halo_send.at[m, 0],
            halo_recv.at[m, 0],
            {"grid": left},
        )
        to_right = remote(
            members.at[m, pl.ds(rows - HALF, HALF)],
            halo.at[m, pl.ds(0, HALF)],
            halo_send.at[m, 1],
            halo_recv.at[m, 1],
            {"grid": right},
        )
        to_left.start()
        to_right.start()
        halo_copies.append((to_left, to_right))

    adj_normed[:LANES, :] = jnp.zeros((LANES, width), F32)
    adj_normed[:nvars, :] = readout_in[...].astype(F32)
    readout[...] = adj_normed[:LANES, :].astype(BF16)
    truth_t[...] = jnp.zeros_like(truth_t)
    truth_t[:nvars, :] = truth_in[...]
    for t in range(tiles):
        part = pl.ds(t * HALF, HALF)
        truth[part, :] = truth_t[:, t * HALF : (t + 1) * HALF].T
        row = jnp.broadcast_to(measure_in[:, t * HALF : (t + 1) * HALF], (HALF, HALF))
        measure[part, :] = row.T
        offset = lax.broadcasted_iota(jnp.int32, (WINDOW, HALF), 0) - HALF
        query = lax.broadcasted_iota(jnp.int32, (WINDOW, HALF), 1)
        point = offset + (first + t * HALF)
        reach = reach_in[:, t * HALF : (t + 1) * HALF]
        inside = (jnp.abs(offset - query) <= reach) & (point >= 0) & (point < total_points)
        bias[t] = jnp.where(inside, 0.0, -1e30).astype(F32)

    def place(m, t):
        return pl.ds((t * count + m) * HALF, HALF)

    for m in range(count):
        loads[m].wait()
        for t in range(tiles):
            normed, _ = normalise(mem[m, t * HALF : (t + 1) * HALF])
            normed_own[place(m, t), :] = normed.astype(BF16)

    def project_own(weight, target, start, factor, c, carry):
        columns = pl.ds(pl.multiple_of(c * COLS, COLS), COLS)
        result = dot(normed_own[...], weight[:, columns])
        if factor is not None:
            result = result * factor
        result = result.astype(BF16)
        for m in range(count):
            for t in range(tiles):
                first_row = (t * count + m) * HALF
                for j in range(2):
                    target[m, 2 * c + j, pl.ds(start + t * HALF, HALF), :] = result[
                        first_row : first_row + HALF, j * LANES : (j + 1) * LANES
                    ]
        return carry

    loads[count].wait()
    own = ((wq, q_s, 0, HEAD**-0.5 * LOG2E), (wk, k_s, HALF, None), (wv, v_s, HALF, None))
    for n, job in enumerate(own):
        if n:
            loads[count + n].wait()
        lax.fori_loop(0, chunks, functools.partial(project_own, *job), 0, unroll=True)
    loads[count + 3].wait()

    def attend(m, some_tiles, p, carry):
        keys = k_s[m, p]
        values = v_s[m, p]
        for t in some_tiles:
            query = per_head(q_s[m, p, t * HALF : (t + 1) * HALF])
            window = slice(t * HALF, t * HALF + WINDOW)
            scores = dot(keys[window], query, NT)
            scores = scores + jnp.concatenate([bias[t]] * 2, axis=1)
            top = jnp.max(scores, axis=0, keepdims=True)
            weights = jnp.exp2(scores - top)
            weights = weights * (1.0 / jnp.sum(weights, axis=0, keepdims=True))
            weights = weights.astype(BF16)
            p_s[m, t, p] = weights
            blended = own_lanes(dot(weights.T, values[window]))
            lanes = pl.ds(pl.multiple_of(p * LANES, LANES), LANES)
            attended[place(m, t), lanes] = blended.astype(BF16)
        return carry

    def attend_all(m, some_tiles):
        lax.fori_loop(0, pairs, functools.partial(attend, m, some_tiles), 0, unroll=True)

    def keys_of_halo(m):
        for copy in halo_copies[m]:
            copy.wait()
        for t in range(2):
            part = pl.ds(t * HALF, HALF)
            normed, _ = normalise(halo[m, part])
            normed_halo[part, :] = normed.astype(BF16)

        def project_halo(c, carry):
            columns = pl.ds(pl.multiple_of(c * COLS, COLS), COLS)
            for weight, target in ((wk, k_s), (wv, v_s)):
                result = dot(normed_halo[...], weight[:, columns]).astype(BF16)
                for j in range(2):
                    lanes = slice(j * LANES, (j + 1) * LANES)
                    target[m, 2 * c + j, pl.ds(0, HALF), :] = result[:HALF, lanes]
                    target[m, 2 * c + j, pl.ds(HALF + rows, HALF), :] = result[HALF:, lanes]
            return carry

        lax.fori_loop(0, chunks, project_halo, 0, unroll=True)

    ens_copies = []

    def forecast(t):
        these = pl.ds(t * count * HALF, count * HALF)

        def mix(c, total):
            columns = pl.ds(pl.multiple_of(c * COLS, COLS), COLS)
            own = [mem[m, t * HALF : (t + 1) * HALF, columns] for m in range(count)]
            mixed = dot(attended[these, :], wo[:, columns])
            mixed = mixed + jnp.concatenate(own, axis=0).astype(F32)
            return total + dot(mixed.astype(BF16), readout[:, columns], NT)

        zero = jnp.zeros((count * HALF, LANES), F32)
        result = lax.fori_loop(0, chunks, mix, zero, unroll=True)
        forecasts[t] = result
        shared[0, t] = result.astype(BF16)
        for slot, device in enumerate(ens_partners):
            copy = remote(
                shared.at[0, t],
                shared.at[slot + 1, t],
                ens_send.at[slot, t],
                ens_recv.at[slot, t],
                device,
            )
            copy.start()
            ens_copies.append(copy)

    for m in range(count - 1):
        keys_of_halo(m)
        attend_all(m, range(tiles))
    keys_of_halo(count - 1)
    for t in range(tiles):
        attend_all(count - 1, (t,))
        forecast(t)

    realizations = count * ens_size
    factor = 1.0 / (realizations - 1)
    real = lax.broadcasted_iota(jnp.int32, (HALF, LANES), 1) < nvars

    def slopes_of(t):
        part = slice(t * HALF, (t + 1) * HALF)
        weight = measure[part, :]
        score = jnp.zeros((HALF, LANES), F32)
        slopes = []
        for m in range(count):
            mine = forecasts[t, m * HALF : (m + 1) * HALF]
            pair_sum = jnp.zeros((HALF, LANES), F32)
            pair_slope = jnp.zeros((HALF, LANES), F32)
            for slot in range(ens_size):
                for other in range(count):
                    theirs = slice(other * HALF, (other + 1) * HALF)
                    if slot == 0 and other == m:
                        continue
                    if slot == 0:
                        gap = mine - forecasts[t, theirs]
                    else:
                        gap = mine - shared[slot, t, theirs].astype(F32)
                    square = gap * gap + SOFT2
                    root = lax.rsqrt(square)
                    pair_sum = pair_sum + square * root
                    pair_slope = pair_slope + gap * root
            gap = mine - truth[part, :]
            square = gap * gap + SOFT2
            root = lax.rsqrt(square)
            score = score + weight * (square * root - 0.5 * factor * pair_sum)
            slopes.append((weight * (gap * root - factor * pair_slope)).astype(BF16))
        return jnp.where(real, score, 0.0), jnp.concatenate(slopes, axis=0)

    def back_to_attended(t, slopes):
        these = pl.ds(t * count * HALF, count * HALF)

        def spread(c, carry):
            columns = pl.ds(pl.multiple_of(c * COLS, COLS), COLS)
            result = dot(slopes, readout[:, columns])
            adj_mixed[these, columns] = result
            adj_mixed_b[these, columns] = result.astype(BF16)
            return carry

        def back_out(c, carry):
            columns = pl.ds(pl.multiple_of(c * COLS, COLS), COLS)
            result = dot(adj_mixed_b[these, :], wo[columns, :], NT)
            adj_attended[these, columns] = result.astype(BF16)
            return carry

        lax.fori_loop(0, chunks, spread, 0, unroll=True)
        lax.fori_loop(0, chunks, back_out, 0, unroll=True)

    score = jnp.zeros((HALF, LANES), F32)
    for t in range(tiles):
        for copy in ens_copies[t * (ens_size - 1) : (t + 1) * (ens_size - 1)]:
            copy.wait()
        scores, slopes = slopes_of(t)
        score = score + scores
        back_to_attended(t, slopes)
    loss_acc[0] = jnp.broadcast_to(jnp.sum(score, keepdims=True), (8, LANES))

    pending = []

    def loss_step(stage):
        if stage > 0 and stage <= len(rounds):
            pending[stage - 1].wait()
            loss_acc[stage] = loss_acc[stage - 1] + loss_in[stage - 1]
        if stage < len(rounds):
            copy = remote(
                loss_acc.at[stage],
                loss_in.at[stage],
                loss_send.at[stage],
                loss_recv.at[stage],
                rounds[stage],
            )
            copy.start()
            pending.append(copy)

    loss_step(0)

    def attend_back(m, p, carry):
        keys = k_s[m, p]
        keys_t = keys.T
        values = v_s[m, p]
        lanes = pl.ds(pl.multiple_of(p * LANES, LANES), LANES)
        key_terms = []
        value_terms = []
        for t in range(tiles):
            mine = place(m, t)
            window = slice(t * HALF, t * HALF + WINDOW)
            query = per_head(q_s[m, p, t * HALF : (t + 1) * HALF])
            adjoint = per_head(adj_attended[mine, lanes])
            weights = p_s[m, t, p]
            wide = weights.astype(F32)
            adj_prob = dot(values[window], adjoint, NT)
            shift = jnp.sum(wide * adj_prob, axis=0, keepdims=True)
            adj_score = (wide * (adj_prob - shift)).astype(BF16)
            adj_query = own_head(dot(keys_t[:, window], adj_score)) * HEAD**-0.5
            dq_s[mine, lanes] = adj_query.astype(BF16)
            key_terms.append(dot(adj_score, query) * LN2)
            value_terms.append(dot(weights, adjoint))
        for terms, own, rim in ((key_terms, dk_s, rim_k), (value_terms, dv_s, rim_v)):
            low, high = terms
            rim[pl.ds(0, HALF), lanes] = low[:HALF].astype(BF16)
            rim[pl.ds(HALF, HALF), lanes] = high[2 * HALF :].astype(BF16)
            both = (low[HALF:] + high[: 2 * HALF]).astype(BF16)
            for t in range(tiles):
                own[place(m, t), lanes] = both[t * HALF : (t + 1) * HALF]
        return carry

    rim_copies = [[] for _ in range(count)]
    for m in range(count):
        lax.fori_loop(0, pairs // 2, functools.partial(attend_back, m), 0, unroll=True)
        loss_step(1 + 3 * m)
        lax.fori_loop(pairs // 2, pairs, functools.partial(attend_back, m), 0, unroll=True)
        loss_step(2 + 3 * m)

        for c in range(chunks):
            columns = slice(c * COLS, (c + 1) * COLS)
            term = dot(rim_k[...], wk[columns, :], NT) + dot(rim_v[...], wv[columns, :], NT)
            rim_out[m, c] = term.astype(BF16)
            for side, device in enumerate((left, right)):
                copy = remote(
                    rim_out.at[m, c, pl.ds(side * HALF, HALF)],
                    rim_in.at[m, c, pl.ds((1 - side) * HALF, HALF)],
                    rim_send.at[m, c, side],
                    rim_recv.at[m, c, side],
                    {"grid": device},
                )
                copy.start()
                rim_copies[m].append(copy)
        loss_step(3 + 3 * m)

    def back_own(c, carry):
        columns = pl.ds(pl.multiple_of(c * COLS, COLS), COLS)
        adj_normed[:, columns] = (
            dot(dq_s[...], wq[columns, :], NT)
            + dot(dk_s[...], wk[columns, :], NT)
            + dot(dv_s[...], wv[columns, :], NT)
        )
        return carry

    lax.fori_loop(0, chunks, back_own, 0, unroll=True)
    for stage in range(3 * count + 1, len(rounds) + 1):
        loss_step(stage)
    loss_out[...] = loss_acc[len(rounds), 0:1, 0:1] * (1.0 / (realizations * total_points * nvars))

    for m in range(count):
        for copy in rim_copies[m]:
            copy.wait()
        for t in range(tiles):
            part = slice(t * HALF, (t + 1) * HALF)
            mine = place(m, t)
            normed, inverse = normalise(mem[m, part])
            rim = jnp.concatenate([rim_in[m, c, part] for c in range(chunks)], axis=1)
            adjoint = adj_normed[mine, :] + rim.astype(F32)
            adjoint = inverse * (
                adjoint
                - jnp.mean(adjoint, axis=-1, keepdims=True)
                - normed * jnp.mean(adjoint * normed, axis=-1, keepdims=True)
            )
            out[m, part] = (adj_mixed[mine, :] + adjoint).astype(BF16)


def per_device(
    ens_size,
    grid_size,
    members,
    observed_truth,
    cell_measure,
    reach,
    w_query,
    w_key,
    w_value,
    w_out,
    readout_coefficients,
):
    count, rows, width = members.shape
    nvars = observed_truth.shape[1]
    pairs = width // LANES
    tiles = rows // HALF
    chunks = width // COLS
    all_rows = count * rows
    stages = ens_size.bit_length() + grid_size.bit_length() - 2
    vmem = pl.BlockSpec(memory_space=pltpu.VMEM)
    anywhere = pl.BlockSpec(memory_space=pl.ANY)
    dma = pltpu.SemaphoreType.DMA
    loss, adjoint = pl.pallas_call(
        functools.partial(kernel, ens_size, grid_size, nvars),
        out_shape=(
            jax.ShapeDtypeStruct((1, 1), F32),
            jax.ShapeDtypeStruct(members.shape, BF16),
        ),
        in_specs=[anywhere, vmem, vmem, vmem, anywhere, anywhere, anywhere, anywhere, vmem],
        out_specs=(vmem, vmem),
        scratch_shapes=[
            pltpu.VMEM((count, rows, width), BF16),
            pltpu.VMEM((count, 2 * HALF, width), BF16),
            pltpu.VMEM((width, width), BF16),
            pltpu.VMEM((width, width), BF16),
            pltpu.VMEM((width, width), BF16),
            pltpu.VMEM((width, width), BF16),
            pltpu.VMEM((LANES, width), BF16),
            pltpu.VMEM((LANES, rows), F32),
            pltpu.VMEM((rows, LANES), F32),
            pltpu.VMEM((rows, LANES), F32),
            pltpu.VMEM((tiles, WINDOW, HALF), F32),
            pltpu.VMEM((all_rows, width), BF16),
            pltpu.VMEM((2 * HALF, width), BF16),
            pltpu.VMEM((count, pairs, rows, LANES), BF16),
            pltpu.VMEM((count, pairs, rows + 2 * HALF, LANES), BF16),
            pltpu.VMEM((count, pairs, rows + 2 * HALF, LANES), BF16),
            pltpu.VMEM((count, tiles, pairs, WINDOW, 2 * HALF), BF16),
            pltpu.VMEM((all_rows, width), BF16),
            pltpu.VMEM((tiles, count * HALF, LANES), F32),
            pltpu.VMEM((ens_size, tiles, count * HALF, LANES), BF16),
            pltpu.VMEM((all_rows, width), F32),
            pltpu.VMEM((all_rows, width), BF16),
            pltpu.VMEM((all_rows, width), BF16),
            pltpu.VMEM((all_rows, width), BF16),
            pltpu.VMEM((all_rows, width), BF16),
            pltpu.VMEM((all_rows, width), BF16),
            pltpu.VMEM((2 * HALF, width), BF16),
            pltpu.VMEM((2 * HALF, width), BF16),
            pltpu.VMEM((count, chunks, 2 * HALF, COLS), BF16),
            pltpu.VMEM((count, chunks, 2 * HALF, COLS), BF16),
            pltpu.VMEM((all_rows, width), F32),
            pltpu.VMEM((stages + 1, 8, LANES), F32),
            pltpu.VMEM((stages, 8, LANES), F32),
            dma((count + 4,)),
            dma((count, 2)),
            dma((count, 2)),
            dma((ens_size - 1, tiles)),
            dma((ens_size - 1, tiles)),
            dma((count, chunks, 2)),
            dma((count, chunks, 2)),
            dma((stages,)),
            dma((stages,)),
        ],
        compiler_params=pltpu.CompilerParams(
            collective_id=0, has_side_effects=True, vmem_limit_bytes=60 * 1024 * 1024
        ),
        cost_estimate=pl.CostEstimate(
            flops=15_000_000_000, bytes_accessed=12_000_000, transcendentals=4_000_000
        ),
    )(
        members,
        observed_truth.T,
        cell_measure.reshape(1, rows),
        reach.reshape(1, rows),
        w_query,
        w_key,
        w_value,
        w_out,
        readout_coefficients.T,
    )
    return loss[0, 0], adjoint


def solution(mesh):
    return jax.shard_map(
        functools.partial(per_device, mesh.shape["ens"], mesh.shape["grid"]),
        mesh=mesh,
        in_specs=(
            P("ens", "grid", None),
            P("grid", None),
            P("grid"),
            P("grid"),
            P(),
            P(),
            P(),
            P(),
            P(),
        ),
        out_specs=(P(), P("ens", "grid", None)),
        check_vma=False,
    )
```

```python
import functools
import math

import jax
import jax.numpy as jnp
from jax import lax
from jax.experimental import pallas as pl
from jax.experimental.pallas import tpu as pltpu
from jax.sharding import PartitionSpec as P

MESH = pl.DeviceIdType.MESH
F32 = jnp.float32
BF16 = jnp.bfloat16
HEAD = 64
HALF = 128
LANES = 128
COLS = 256
WINDOW = 3 * HALF
EPS = 1e-05
SOFT2 = 0.01
SOFT = 0.1
LOG2E = math.log2(math.e)
LN2 = math.log(2.0)

NN = (((1,), (0,)), ((), ()))
NT = (((1,), (1,)), ((), ()))


def dot(a, b, dims=NN):
    return lax.dot_general(a, b, dims, preferred_element_type=F32)


def flip(index, bits):
    turned = index
    for bit in (1 << b for b in range(bits.bit_length())):
        if bits & bit:
            turned = turned + bit * (1 - 2 * ((index // bit) % 2))
    return turned


def tree_sum(terms):
    while len(terms) > 1:
        terms = [terms[n] + terms[n + 1] for n in range(0, len(terms), 2)]
    return terms[0]


def loss_groups(ens_size, grid_size):
    groups = [("ens", tuple(range(1, ens_size)))]
    low = 1
    while low < grid_size:
        high = min(8, grid_size // low)
        groups.append(("grid", tuple(low * n for n in range(1, high))))
        low *= high
    return groups


def normalise(block):
    values = block.astype(F32)
    centred = values - jnp.mean(values, axis=-1, keepdims=True)
    inverse = lax.rsqrt(jnp.mean(centred * centred, axis=-1, keepdims=True) + EPS)
    return centred * inverse, inverse


def per_head(pair):
    low = lax.broadcasted_iota(jnp.int32, pair.shape, 1) < HEAD
    zero = jnp.zeros_like(pair)
    return jnp.concatenate([jnp.where(low, pair, zero), jnp.where(low, zero, pair)], axis=0)


def own_lanes(tall):
    low = lax.broadcasted_iota(jnp.int32, (HALF, LANES), 1) < HEAD
    return jnp.where(low, tall[:HALF], tall[HALF:])


def own_head(wide):
    both = jnp.concatenate([wide[:HEAD, :HALF], wide[HEAD:, HALF:]], axis=0)
    return both.T


def kernel(
    ens_size,
    grid_size,
    nvars,
    members,
    truth_in,
    measure_in,
    reach_in,
    w_query,
    w_key,
    w_value,
    w_out,
    readout_in,
    loss_out,
    out,
    mem,
    halo,
    wq,
    wk,
    wv,
    wo,
    readout,
    truth_t,
    truth,
    measure,
    bias,
    normed_own,
    normed_wide,
    inverse_own,
    normed_halo,
    q_s,
    k_s,
    v_s,
    p_s,
    ds_s,
    attended,
    forecasts,
    shared,
    folded,
    slopes,
    adj_mixed,
    adj_attended,
    dq_s,
    dk_s,
    dv_s,
    rim_k,
    rim_v,
    rim_out,
    rim_in,
    adj_normed,
    loss_acc,
    loss_in,
    load_sem,
    halo_send,
    halo_recv,
    ens_send,
    ens_recv,
    rim_send,
    rim_recv,
    loss_send,
    loss_recv,
):
    count, rows, width = members.shape
    pairs = width // LANES
    chunks = width // COLS
    tiles = rows // HALF
    ens = lax.axis_index("ens")
    grid = lax.axis_index("grid")
    right = lax.rem(grid + 1, grid_size)
    left = lax.rem(grid + grid_size - 1, grid_size)
    first = grid * rows
    total_points = rows * grid_size
    ens_partners = [{"ens": flip(ens, n)} for n in range(1, ens_size)]
    position = {"ens": ens, "grid": grid}
    rounds = [
        [{axis: flip(position[axis], n)} for n in numbers]
        for axis, numbers in loss_groups(ens_size, grid_size)
    ]

    def remote(source, target, send, recv, device):
        return pltpu.make_async_remote_copy(
            src_ref=source,
            dst_ref=target,
            send_sem=send,
            recv_sem=recv,
            device_id=device,
            device_id_type=MESH,
        )

    loads = []
    for m in range(count):
        loads.append(pltpu.make_async_copy(members.at[m], mem.at[m], load_sem.at[m]))
    for n, (source, target) in enumerate(((w_query, wq), (w_key, wk), (w_value, wv), (w_out, wo))):
        loads.append(pltpu.make_async_copy(source, target, load_sem.at[count + n]))
    for load in loads:
        load.start()

    barrier = pltpu.get_barrier_semaphore()
    greeted = [{"grid": left}, {"grid": right}] + [device for group in rounds for device in group]
    for device in greeted:
        pl.semaphore_signal(barrier, inc=1, device_id=device, device_id_type=MESH)
    pl.semaphore_wait(barrier, len(greeted))

    halo_copies = []
    for m in range(count):
        to_left = remote(
            members.at[m, pl.ds(0, HALF)],
            halo.at[m, pl.ds(HALF, HALF)],
            halo_send.at[m, 0],
            halo_recv.at[m, 0],
            {"grid": left},
        )
        to_right = remote(
            members.at[m, pl.ds(rows - HALF, HALF)],
            halo.at[m, pl.ds(0, HALF)],
            halo_send.at[m, 1],
            halo_recv.at[m, 1],
            {"grid": right},
        )
        halo_copies.append((to_left, to_right))
    for copy in halo_copies[0]:
        copy.start()

    adj_normed[:LANES, :] = jnp.zeros((LANES, width), F32)
    adj_normed[:nvars, :] = readout_in[...].astype(F32)
    readout[...] = adj_normed[:LANES, :].astype(BF16)
    truth_t[...] = jnp.zeros_like(truth_t)
    truth_t[:nvars, :] = truth_in[...]
    for t in range(tiles):
        part = pl.ds(t * HALF, HALF)
        truth[part, :] = truth_t[:, t * HALF : (t + 1) * HALF].T
        row = jnp.broadcast_to(measure_in[:, t * HALF : (t + 1) * HALF], (HALF, HALF))
        measure[part, :] = row.T
        offset = lax.broadcasted_iota(jnp.int32, (WINDOW, HALF), 0) - HALF
        query = lax.broadcasted_iota(jnp.int32, (WINDOW, HALF), 1)
        point = offset + (first + t * HALF)
        reach = reach_in[:, t * HALF : (t + 1) * HALF]
        inside = (jnp.abs(offset - query) <= reach) & (point >= 0) & (point < total_points)
        bias[t] = jnp.where(inside, 0.0, -1e30).astype(F32)

    def place(m, t):
        return pl.ds((t * count + m) * HALF, HALF)

    for m in range(count):
        loads[m].wait()
        for t in range(tiles):
            normed, inverse = normalise(mem[m, t * HALF : (t + 1) * HALF])
            normed_own[place(m, t), :] = normed.astype(BF16)
            normed_wide[place(m, t), :] = normed
            inverse_own[place(m, t), :] = jnp.broadcast_to(inverse, (HALF, LANES))

    for pair in halo_copies[1:]:
        for copy in pair:
            copy.start()

    def project_own(weight, target, start, factor, c, carry):
        columns = pl.ds(pl.multiple_of(c * COLS, COLS), COLS)
        result = dot(normed_own[...], weight[:, columns])
        if factor is not None:
            result = result * factor
        result = result.astype(BF16)
        for m in range(count):
            for t in range(tiles):
                first_row = (t * count + m) * HALF
                for j in range(2):
                    target[m, 2 * c + j, pl.ds(start + t * HALF, HALF), :] = result[
                        first_row : first_row + HALF, j * LANES : (j + 1) * LANES
                    ]
        return carry

    loads[count].wait()
    own = ((wq, q_s, 0, HEAD**-0.5 * LOG2E), (wk, k_s, HALF, None), (wv, v_s, HALF, None))
    for n, job in enumerate(own):
        if n:
            loads[count + n].wait()
        lax.fori_loop(0, chunks, functools.partial(project_own, *job), 0, unroll=True)

    def attend(m, some_tiles, p, carry):
        keys = k_s[m, p]
        values = v_s[m, p]
        for t in some_tiles:
            query = per_head(q_s[m, p, t * HALF : (t + 1) * HALF])
            window = slice(t * HALF, t * HALF + WINDOW)
            scores = dot(keys[window], query, NT)
            scores = scores + jnp.concatenate([bias[t]] * 2, axis=1)
            top = jnp.max(scores, axis=0, keepdims=True)
            weights = jnp.exp2(scores - top)
            weights = weights * (1.0 / jnp.sum(weights, axis=0, keepdims=True))
            weights = weights.astype(BF16)
            p_s[m, t, p] = weights
            blended = own_lanes(dot(weights.T, values[window]))
            lanes = pl.ds(pl.multiple_of(p * LANES, LANES), LANES)
            attended[place(m, t), lanes] = blended.astype(BF16)
        return carry

    def attend_all(m, some_tiles):
        lax.fori_loop(0, pairs, functools.partial(attend, m, some_tiles), 0, unroll=True)

    def keys_of_halo(m):
        for copy in halo_copies[m]:
            copy.wait()
        for t in range(2):
            part = pl.ds(t * HALF, HALF)
            normed, _ = normalise(halo[m, part])
            normed_halo[part, :] = normed.astype(BF16)

        def project_halo(c, carry):
            columns = pl.ds(pl.multiple_of(c * COLS, COLS), COLS)
            for weight, target in ((wk, k_s), (wv, v_s)):
                result = dot(normed_halo[...], weight[:, columns]).astype(BF16)
                for j in range(2):
                    lanes = slice(j * LANES, (j + 1) * LANES)
                    target[m, 2 * c + j, pl.ds(0, HALF), :] = result[:HALF, lanes]
                    target[m, 2 * c + j, pl.ds(HALF + rows, HALF), :] = result[HALF:, lanes]
            return carry

        lax.fori_loop(0, chunks, project_halo, 0, unroll=True)

    ens_copies = [[] for _ in range(tiles)]

    def fold_readout(c, carry):
        part = pl.ds(pl.multiple_of(c * COLS, COLS), COLS)
        folded[part, :] = dot(wo[part, :], readout[...], NT).astype(BF16)
        return carry

    def forecast(m, t):
        these = pl.ds(m * HALF, HALF)
        result = forecasts[t, these, :] + dot(attended[place(m, t), :], folded[...])
        forecasts[t, these, :] = result
        shared[0, t, m] = result.astype(BF16)
        for slot, device in enumerate(ens_partners):
            copy = remote(
                shared.at[0, t, m],
                shared.at[slot + 1, t, m],
                ens_send.at[slot, t, m],
                ens_recv.at[slot, t, m],
                device,
            )
            copy.start()
            ens_copies[t].append(copy)

    keys_of_halo(0)
    attend_all(0, range(tiles))
    loads[count + 3].wait()
    lax.fori_loop(0, chunks, fold_readout, 0, unroll=True)
    for m in range(count):
        base = dot(mem[m], readout[...], NT)
        for t in range(tiles):
            forecasts[t, m * HALF : (m + 1) * HALF, :] = base[t * HALF : (t + 1) * HALF]
    for t in range(tiles):
        forecast(0, t)
    for m in range(1, count):
        keys_of_halo(m)
        for t in range(tiles):
            attend_all(m, (t,))
            forecast(m, t)

    realizations = count * ens_size
    factor = 1.0 / (realizations - 1)
    def slopes_of(t):
        part = slice(t * HALF, (t + 1) * HALF)
        weight = measure[part, :]
        score = jnp.zeros((HALF, LANES), F32)
        parts = []
        for m in range(count):
            mine = forecasts[t, m * HALF : (m + 1) * HALF]
            pair_sum = jnp.zeros((HALF, LANES), F32)
            pair_slope = jnp.zeros((HALF, LANES), F32)
            for slot in range(ens_size):
                for other in range(count):
                    theirs = slice(other * HALF, (other + 1) * HALF)
                    if slot == 0 and other == m:
                        continue
                    if slot == 0:
                        gap = mine - forecasts[t, theirs]
                    else:
                        gap = mine - shared[slot, t, other].astype(F32)
                    square = gap * gap + SOFT2
                    root = lax.rsqrt(square)
                    pair_sum = pair_sum + square * root
                    pair_slope = pair_slope + gap * root
            gap = mine - truth[part, :]
            square = gap * gap + SOFT2
            root = lax.rsqrt(square)
            score = score + weight * (square * root - 0.5 * factor * pair_sum)
            parts.append((weight * (gap * root - factor * pair_slope)).astype(BF16))
        return score, jnp.concatenate(parts, axis=0)

    def back_to_attended(t):
        for copy in ens_copies[t]:
            copy.wait()
        score, result = slopes_of(t)
        these = pl.ds(t * count * HALF, count * HALF)
        slopes[these, :] = result

        def back_out(c, carry):
            columns = pl.ds(pl.multiple_of(c * COLS, COLS), COLS)
            adj_attended[these, columns] = dot(result, folded[columns, :], NT).astype(BF16)
            return carry

        lax.fori_loop(0, chunks, back_out, 0, unroll=True)
        return score

    pending = []

    def loss_start(stage):
        copies = []
        for n, device in enumerate(rounds[stage]):
            copy = remote(
                loss_acc.at[stage],
                loss_in.at[stage, n],
                loss_send.at[stage, n],
                loss_recv.at[stage, n],
                device,
            )
            copy.start()
            copies.append(copy)
        pending.append(copies)

    def loss_finish(stage):
        for copy in pending[stage]:
            copy.wait()
        terms = [loss_acc[stage]] + [loss_in[stage, n] for n in range(len(rounds[stage]))]
        loss_acc[stage + 1] = tree_sum(terms)

    def attend_back(m, p, carry):
        keys = k_s[m, p]
        values = v_s[m, p]
        lanes = pl.ds(pl.multiple_of(p * LANES, LANES), LANES)
        key_terms = []
        value_terms = []
        for t in range(tiles):
            window = slice(t * HALF, t * HALF + WINDOW)
            query = per_head(q_s[m, p, t * HALF : (t + 1) * HALF])
            adjoint = per_head(adj_attended[place(m, t), lanes])
            weights = p_s[m, t, p]
            wide = weights.astype(F32)
            adj_prob = dot(values[window], adjoint, NT)
            shift = jnp.sum(wide * adj_prob, axis=0, keepdims=True)
            adj_score = (wide * (adj_prob - shift)).astype(BF16)
            ds_s[m, t, p] = adj_score
            key_terms.append(dot(adj_score, query) * LN2)
            value_terms.append(dot(weights, adjoint))
        for terms, own, rim in ((key_terms, dk_s, rim_k), (value_terms, dv_s, rim_v)):
            low, high = terms
            rim[pl.ds(0, HALF), lanes] = low[:HALF].astype(BF16)
            rim[pl.ds(HALF, HALF), lanes] = high[2 * HALF :].astype(BF16)
            both = (low[HALF:] + high[: 2 * HALF]).astype(BF16)
            for t in range(tiles):
                own[place(m, t), lanes] = both[t * HALF : (t + 1) * HALF]
        return carry

    def query_back(m, p, carry):
        keys_t = k_s[m, p].T
        lanes = pl.ds(pl.multiple_of(p * LANES, LANES), LANES)
        for t in range(tiles):
            window = slice(t * HALF, t * HALF + WINDOW)
            adj_query = own_head(dot(keys_t[:, window], ds_s[m, t, p])) * HEAD**-0.5
            dq_s[place(m, t), lanes] = adj_query.astype(BF16)
        return carry

    real = lax.broadcasted_iota(jnp.int32, (HALF, LANES), 1) < nvars
    score = sum(back_to_attended(t) for t in range(tiles))
    score = jnp.where(real, score, 0.0)
    loss_acc[0] = jnp.broadcast_to(jnp.sum(score, keepdims=True), (8, LANES))
    loss_start(0)
    rim_copies = [[] for _ in range(count)]
    for m in range(count):
        lax.fori_loop(0, pairs, functools.partial(attend_back, m), 0, unroll=True)
        if m == 1:
            loss_finish(1)
            loss_start(2)

        for c in range(chunks):
            columns = slice(c * COLS, (c + 1) * COLS)
            term = dot(rim_k[...], wk[columns, :], NT) + dot(rim_v[...], wv[columns, :], NT)
            rim_out[m, c] = term.astype(BF16)
            for side, device in enumerate((left, right)):
                copy = remote(
                    rim_out.at[m, c, pl.ds(side * HALF, HALF)],
                    rim_in.at[m, c, pl.ds((1 - side) * HALF, HALF)],
                    rim_send.at[m, c, side],
                    rim_recv.at[m, c, side],
                    {"grid": device},
                )
                copy.start()
                rim_copies[m].append(copy)
        if m == 0:
            loss_finish(0)
            loss_start(1)

    for m in range(count):
        lax.fori_loop(0, pairs, functools.partial(query_back, m), 0, unroll=True)
    def back_own(c, carry):
        columns = pl.ds(pl.multiple_of(c * COLS, COLS), COLS)
        adj_normed[:, columns] = (
            dot(dq_s[...], wq[columns, :], NT)
            + dot(dk_s[...], wk[columns, :], NT)
            + dot(dv_s[...], wv[columns, :], NT)
        )
        adj_mixed[:, columns] = dot(slopes[...], readout[:, columns])
        return carry

    lax.fori_loop(0, chunks, back_own, 0, unroll=True)
    loss_finish(2)
    loss_out[...] = loss_acc[3, 0:1, 0:1] * (1.0 / (realizations * total_points * nvars))

    for m in range(count):
        for copy in rim_copies[m]:
            copy.wait()
        for t in range(tiles):
            part = slice(t * HALF, (t + 1) * HALF)
            mine = place(m, t)
            normed = normed_wide[mine, :]
            inverse = inverse_own[mine, :1]
            rim = jnp.concatenate([rim_in[m, c, part] for c in range(chunks)], axis=1)
            adjoint = adj_normed[mine, :] + rim.astype(F32)
            adjoint = inverse * (
                adjoint
                - jnp.mean(adjoint, axis=-1, keepdims=True)
                - normed * jnp.mean(adjoint * normed, axis=-1, keepdims=True)
            )
            out[m, part] = (adj_mixed[mine, :] + adjoint).astype(BF16)


def per_device(
    ens_size,
    grid_size,
    members,
    observed_truth,
    cell_measure,
    reach,
    w_query,
    w_key,
    w_value,
    w_out,
    readout_coefficients,
):
    count, rows, width = members.shape
    nvars = observed_truth.shape[1]
    pairs = width // LANES
    tiles = rows // HALF
    chunks = width // COLS
    all_rows = count * rows
    groups = loss_groups(ens_size, grid_size)
    stages = len(groups)
    most = max(len(numbers) for _, numbers in groups)
    vmem = pl.BlockSpec(memory_space=pltpu.VMEM)
    anywhere = pl.BlockSpec(memory_space=pl.ANY)
    dma = pltpu.SemaphoreType.DMA
    loss, adjoint = pl.pallas_call(
        functools.partial(kernel, ens_size, grid_size, nvars),
        out_shape=(
            jax.ShapeDtypeStruct((1, 1), F32),
            jax.ShapeDtypeStruct(members.shape, BF16),
        ),
        in_specs=[anywhere, vmem, vmem, vmem, anywhere, anywhere, anywhere, anywhere, vmem],
        out_specs=(vmem, vmem),
        scratch_shapes=[
            pltpu.VMEM((count, rows, width), BF16),
            pltpu.VMEM((count, 2 * HALF, width), BF16),
            pltpu.VMEM((width, width), BF16),
            pltpu.VMEM((width, width), BF16),
            pltpu.VMEM((width, width), BF16),
            pltpu.VMEM((width, width), BF16),
            pltpu.VMEM((LANES, width), BF16),
            pltpu.VMEM((LANES, rows), F32),
            pltpu.VMEM((rows, LANES), F32),
            pltpu.VMEM((rows, LANES), F32),
            pltpu.VMEM((tiles, WINDOW, HALF), F32),
            pltpu.VMEM((all_rows, width), BF16),
            pltpu.VMEM((all_rows, width), F32),
            pltpu.VMEM((all_rows, LANES), F32),
            pltpu.VMEM((2 * HALF, width), BF16),
            pltpu.VMEM((count, pairs, rows, LANES), BF16),
            pltpu.VMEM((count, pairs, rows + 2 * HALF, LANES), BF16),
            pltpu.VMEM((count, pairs, rows + 2 * HALF, LANES), BF16),
            pltpu.VMEM((count, tiles, pairs, WINDOW, 2 * HALF), BF16),
            pltpu.VMEM((count, tiles, pairs, WINDOW, 2 * HALF), BF16),
            pltpu.VMEM((all_rows, width), BF16),
            pltpu.VMEM((tiles, count * HALF, LANES), F32),
            pltpu.VMEM((ens_size, tiles, count, HALF, LANES), BF16),
            pltpu.VMEM((width, LANES), BF16),
            pltpu.VMEM((all_rows, LANES), BF16),
            pltpu.VMEM((all_rows, width), F32),
            pltpu.VMEM((all_rows, width), BF16),
            pltpu.VMEM((all_rows, width), BF16),
            pltpu.VMEM((all_rows, width), BF16),
            pltpu.VMEM((all_rows, width), BF16),
            pltpu.VMEM((2 * HALF, width), BF16),
            pltpu.VMEM((2 * HALF, width), BF16),
            pltpu.VMEM((count, chunks, 2 * HALF, COLS), BF16),
            pltpu.VMEM((count, chunks, 2 * HALF, COLS), BF16),
            pltpu.VMEM((all_rows, width), F32),
            pltpu.VMEM((stages + 1, 8, LANES), F32),
            pltpu.VMEM((stages, most, 8, LANES), F32),
            dma((count + 4,)),
            dma((count, 2)),
            dma((count, 2)),
            dma((ens_size - 1, tiles, count)),
            dma((ens_size - 1, tiles, count)),
            dma((count, chunks, 2)),
            dma((count, chunks, 2)),
            dma((stages, most)),
            dma((stages, most)),
        ],
        compiler_params=pltpu.CompilerParams(
            collective_id=0, has_side_effects=True, vmem_limit_bytes=60 * 1024 * 1024
        ),
        cost_estimate=pl.CostEstimate(
            flops=15_000_000_000, bytes_accessed=12_000_000, transcendentals=4_000_000
        ),
    )(
        members,
        observed_truth.T,
        cell_measure.reshape(1, rows),
        reach.reshape(1, rows),
        w_query,
        w_key,
        w_value,
        w_out,
        readout_coefficients.T,
    )
    return loss[0, 0], adjoint


def solution(mesh):
    return jax.shard_map(
        functools.partial(per_device, mesh.shape["ens"], mesh.shape["grid"]),
        mesh=mesh,
        in_specs=(
            P("ens", "grid", None),
            P("grid", None),
            P("grid"),
            P("grid"),
            P(),
            P(),
            P(),
            P(),
            P(),
        ),
        out_specs=(P(), P("ens", "grid", None)),
        check_vma=False,
    )
```

```python
import functools
import math

import jax
import jax.numpy as jnp
from jax import lax
from jax.experimental import pallas as pl
from jax.experimental.pallas import tpu as pltpu
from jax.sharding import PartitionSpec as P

MESH = pl.DeviceIdType.MESH
F32 = jnp.float32
BF16 = jnp.bfloat16
HEAD = 64
HALF = 128
LANES = 128
COLS = 256
WINDOW = 3 * HALF
EPS = 1e-05
SOFT2 = 0.01
SOFT = 0.1
LOG2E = math.log2(math.e)
LN2 = math.log(2.0)

NN = (((1,), (0,)), ((), ()))
NT = (((1,), (1,)), ((), ()))


def dot(a, b, dims=NN):
    return lax.dot_general(a, b, dims, preferred_element_type=F32)


def flip(index, bits):
    turned = index
    for bit in (1 << b for b in range(bits.bit_length())):
        if bits & bit:
            turned = turned + bit * (1 - 2 * ((index // bit) % 2))
    return turned


def tree_sum(terms):
    while len(terms) > 1:
        terms = [terms[n] + terms[n + 1] for n in range(0, len(terms), 2)]
    return terms[0]


def loss_groups(ens_size, grid_size):
    groups = [("ens", tuple(range(1, ens_size)))]
    low = 1
    while low < grid_size:
        high = min(8, grid_size // low)
        groups.append(("grid", tuple(low * n for n in range(1, high))))
        low *= high
    return groups


def normalise(block):
    values = block.astype(F32)
    centred = values - jnp.mean(values, axis=-1, keepdims=True)
    inverse = lax.rsqrt(jnp.mean(centred * centred, axis=-1, keepdims=True) + EPS)
    return centred * inverse, inverse


def per_head(pair):
    low = lax.broadcasted_iota(jnp.int32, pair.shape, 1) < HEAD
    zero = jnp.zeros_like(pair)
    return jnp.concatenate([jnp.where(low, pair, zero), jnp.where(low, zero, pair)], axis=0)


def own_lanes(tall):
    low = lax.broadcasted_iota(jnp.int32, (HALF, LANES), 1) < HEAD
    return jnp.where(low, tall[:HALF], tall[HALF:])


def own_head(wide):
    both = jnp.concatenate([wide[:HEAD, :HALF], wide[HEAD:, HALF:]], axis=0)
    return both.T


def kernel(
    ens_size,
    grid_size,
    nvars,
    members,
    truth_in,
    measure_in,
    reach_in,
    w_query,
    w_key,
    w_value,
    w_out,
    readout_in,
    loss_out,
    out,
    mem,
    halo,
    wq,
    wk,
    wv,
    wo,
    readout,
    truth_t,
    truth,
    measure,
    bias,
    normed_own,
    normed_wide,
    inverse_own,
    normed_halo,
    q_s,
    k_s,
    v_s,
    p_s,
    ds_s,
    attended,
    forecasts,
    shared,
    folded,
    slopes,
    adj_mixed,
    adj_attended,
    dq_s,
    dk_s,
    dv_s,
    rim_k,
    rim_v,
    rim_out,
    rim_in,
    adj_normed,
    result,
    loss_acc,
    loss_in,
    load_sem,
    out_sem,
    halo_send,
    halo_recv,
    ens_send,
    ens_recv,
    rim_send,
    rim_recv,
    loss_send,
    loss_recv,
):
    count, rows, width = members.shape
    pairs = width // LANES
    chunks = width // COLS
    tiles = rows // HALF
    ens = lax.axis_index("ens")
    grid = lax.axis_index("grid")
    right = lax.rem(grid + 1, grid_size)
    left = lax.rem(grid + grid_size - 1, grid_size)
    first = grid * rows
    total_points = rows * grid_size
    ens_partners = [{"ens": flip(ens, n)} for n in range(1, ens_size)]
    position = {"ens": ens, "grid": grid}
    rounds = [
        [{axis: flip(position[axis], n)} for n in numbers]
        for axis, numbers in loss_groups(ens_size, grid_size)
    ]

    def remote(source, target, send, recv, device):
        return pltpu.make_async_remote_copy(
            src_ref=source,
            dst_ref=target,
            send_sem=send,
            recv_sem=recv,
            device_id=device,
            device_id_type=MESH,
        )

    loads = []
    for m in range(count):
        loads.append(pltpu.make_async_copy(members.at[m], mem.at[m], load_sem.at[m]))
    for n, (source, target) in enumerate(((w_query, wq), (w_key, wk), (w_value, wv), (w_out, wo))):
        loads.append(pltpu.make_async_copy(source, target, load_sem.at[count + n]))
    for load in loads:
        load.start()

    barrier = pltpu.get_barrier_semaphore()
    greeted = [{"grid": left}, {"grid": right}] + [device for group in rounds for device in group]
    for device in greeted:
        pl.semaphore_signal(barrier, inc=1, device_id=device, device_id_type=MESH)
    pl.semaphore_wait(barrier, len(greeted))

    halo_copies = []
    for m in range(count):
        to_left = remote(
            members.at[m, pl.ds(0, HALF)],
            halo.at[m, pl.ds(HALF, HALF)],
            halo_send.at[m, 0],
            halo_recv.at[m, 0],
            {"grid": left},
        )
        to_right = remote(
            members.at[m, pl.ds(rows - HALF, HALF)],
            halo.at[m, pl.ds(0, HALF)],
            halo_send.at[m, 1],
            halo_recv.at[m, 1],
            {"grid": right},
        )
        halo_copies.append((to_left, to_right))
    for copy in halo_copies[0]:
        copy.start()

    adj_normed[:LANES, :] = jnp.zeros((LANES, width), F32)
    adj_normed[:nvars, :] = readout_in[...].astype(F32)
    readout[...] = adj_normed[:LANES, :].astype(BF16)
    truth_t[...] = jnp.zeros_like(truth_t)
    truth_t[:nvars, :] = truth_in[...]
    for t in range(tiles):
        part = pl.ds(t * HALF, HALF)
        truth[part, :] = truth_t[:, t * HALF : (t + 1) * HALF].T
        row = jnp.broadcast_to(measure_in[:, t * HALF : (t + 1) * HALF], (HALF, HALF))
        measure[part, :] = row.T
        offset = lax.broadcasted_iota(jnp.int32, (WINDOW, HALF), 0) - HALF
        query = lax.broadcasted_iota(jnp.int32, (WINDOW, HALF), 1)
        point = offset + (first + t * HALF)
        reach = reach_in[:, t * HALF : (t + 1) * HALF]
        inside = (jnp.abs(offset - query) <= reach) & (point >= 0) & (point < total_points)
        bias[t] = jnp.where(inside, 0.0, -1e30).astype(F32)

    def place(m, t):
        return pl.ds((t * count + m) * HALF, HALF)

    for m in range(count):
        loads[m].wait()
        if m:
            for copy in halo_copies[m]:
                copy.start()
        for t in range(tiles):
            normed, inverse = normalise(mem[m, t * HALF : (t + 1) * HALF])
            normed_own[place(m, t), :] = normed.astype(BF16)
            normed_wide[place(m, t), :] = normed
            inverse_own[place(m, t), :] = jnp.broadcast_to(inverse, (HALF, LANES))

    def project_own(weight, target, start, factor, c, carry):
        columns = pl.ds(pl.multiple_of(c * COLS, COLS), COLS)
        result = dot(normed_own[...], weight[:, columns])
        if factor is not None:
            result = result * factor
        result = result.astype(BF16)
        for m in range(count):
            for t in range(tiles):
                first_row = (t * count + m) * HALF
                for j in range(2):
                    target[m, 2 * c + j, pl.ds(start + t * HALF, HALF), :] = result[
                        first_row : first_row + HALF, j * LANES : (j + 1) * LANES
                    ]
        return carry

    loads[count].wait()
    own = ((wq, q_s, 0, HEAD**-0.5 * LOG2E), (wk, k_s, HALF, None), (wv, v_s, HALF, None))
    for n, job in enumerate(own):
        if n:
            loads[count + n].wait()
        lax.fori_loop(0, chunks, functools.partial(project_own, *job), 0, unroll=True)

    def attend(m, some_tiles, p, carry):
        keys = k_s[m, p]
        values = v_s[m, p]
        for t in some_tiles:
            query = per_head(q_s[m, p, t * HALF : (t + 1) * HALF])
            window = slice(t * HALF, t * HALF + WINDOW)
            scores = dot(keys[window], query, NT)
            scores = scores + jnp.concatenate([bias[t]] * 2, axis=1)
            top = jnp.max(scores, axis=0, keepdims=True)
            weights = jnp.exp2(scores - top)
            weights = weights * (1.0 / jnp.sum(weights, axis=0, keepdims=True))
            weights = weights.astype(BF16)
            p_s[m, t, p] = weights
            blended = own_lanes(dot(weights.T, values[window]))
            lanes = pl.ds(pl.multiple_of(p * LANES, LANES), LANES)
            attended[place(m, t), lanes] = blended.astype(BF16)
        return carry

    def attend_all(m, some_tiles):
        lax.fori_loop(0, pairs, functools.partial(attend, m, some_tiles), 0, unroll=True)

    def keys_of_halo(m):
        for copy in halo_copies[m]:
            copy.wait()
        for t in range(2):
            part = pl.ds(t * HALF, HALF)
            normed, _ = normalise(halo[m, part])
            normed_halo[part, :] = normed.astype(BF16)

        def project_halo(c, carry):
            columns = pl.ds(pl.multiple_of(c * COLS, COLS), COLS)
            for weight, target in ((wk, k_s), (wv, v_s)):
                result = dot(normed_halo[...], weight[:, columns]).astype(BF16)
                for j in range(2):
                    lanes = slice(j * LANES, (j + 1) * LANES)
                    target[m, 2 * c + j, pl.ds(0, HALF), :] = result[:HALF, lanes]
                    target[m, 2 * c + j, pl.ds(HALF + rows, HALF), :] = result[HALF:, lanes]
            return carry

        lax.fori_loop(0, chunks, project_halo, 0, unroll=True)

    ens_copies = [[] for _ in range(tiles)]

    def fold_readout(c, carry):
        part = pl.ds(pl.multiple_of(c * COLS, COLS), COLS)
        folded[part, :] = dot(wo[part, :], readout[...], NT).astype(BF16)
        return carry

    def forecast(m, t):
        these = pl.ds(m * HALF, HALF)
        result = forecasts[t, these, :] + dot(attended[place(m, t), :], folded[...])
        forecasts[t, these, :] = result
        shared[0, t, m] = result.astype(BF16)
        for slot in reversed(range(len(ens_partners))):
            copy = remote(
                shared.at[0, t, m],
                shared.at[slot + 1, t, m],
                ens_send.at[slot, t, m],
                ens_recv.at[slot, t, m],
                ens_partners[slot],
            )
            copy.start()
            ens_copies[t].append(copy)

    keys_of_halo(0)
    attend_all(0, range(tiles))
    loads[count + 3].wait()
    lax.fori_loop(0, chunks, fold_readout, 0, unroll=True)
    for m in range(count):
        base = dot(mem[m], readout[...], NT)
        for t in range(tiles):
            forecasts[t, m * HALF : (m + 1) * HALF, :] = base[t * HALF : (t + 1) * HALF]
    for t in range(tiles):
        forecast(0, t)
    for m in range(1, count):
        keys_of_halo(m)
        for t in range(tiles):
            attend_all(m, (t,))
            forecast(m, t)

    realizations = count * ens_size
    factor = 1.0 / (realizations - 1)
    def slopes_of(t):
        part = slice(t * HALF, (t + 1) * HALF)
        weight = measure[part, :]
        score = jnp.zeros((HALF, LANES), F32)
        parts = []
        for m in range(count):
            mine = forecasts[t, m * HALF : (m + 1) * HALF]
            pair_sum = jnp.zeros((HALF, LANES), F32)
            pair_slope = jnp.zeros((HALF, LANES), F32)
            for slot in range(ens_size):
                for other in range(count):
                    theirs = slice(other * HALF, (other + 1) * HALF)
                    if slot == 0 and other == m:
                        continue
                    if slot == 0:
                        gap = mine - forecasts[t, theirs]
                    else:
                        gap = mine - shared[slot, t, other].astype(F32)
                    square = gap * gap + SOFT2
                    root = lax.rsqrt(square)
                    pair_sum = pair_sum + square * root
                    pair_slope = pair_slope + gap * root
            gap = mine - truth[part, :]
            square = gap * gap + SOFT2
            root = lax.rsqrt(square)
            score = score + weight * (square * root - 0.5 * factor * pair_sum)
            parts.append((weight * (gap * root - factor * pair_slope)).astype(BF16))
        return score, jnp.concatenate(parts, axis=0)

    def back_to_attended(t):
        for copy in ens_copies[t]:
            copy.wait()
        score, result = slopes_of(t)
        these = pl.ds(t * count * HALF, count * HALF)
        slopes[these, :] = result

        def back_out(c, carry):
            columns = pl.ds(pl.multiple_of(c * COLS, COLS), COLS)
            adj_attended[these, columns] = dot(result, folded[columns, :], NT).astype(BF16)
            return carry

        lax.fori_loop(0, chunks, back_out, 0, unroll=True)
        return score

    pending = []

    def loss_start(stage):
        copies = []
        for n, device in enumerate(rounds[stage]):
            copy = remote(
                loss_acc.at[stage],
                loss_in.at[stage, n],
                loss_send.at[stage, n],
                loss_recv.at[stage, n],
                device,
            )
            copy.start()
            copies.append(copy)
        pending.append(copies)

    def loss_finish(stage):
        for copy in pending[stage]:
            copy.wait()
        terms = [loss_acc[stage]] + [loss_in[stage, n] for n in range(len(rounds[stage]))]
        loss_acc[stage + 1] = tree_sum(terms)

    def attend_back(m, p, carry):
        keys = k_s[m, p]
        values = v_s[m, p]
        lanes = pl.ds(pl.multiple_of(p * LANES, LANES), LANES)
        key_terms = []
        value_terms = []
        for t in range(tiles):
            window = slice(t * HALF, t * HALF + WINDOW)
            query = per_head(q_s[m, p, t * HALF : (t + 1) * HALF])
            adjoint = per_head(adj_attended[place(m, t), lanes])
            weights = p_s[m, t, p]
            wide = weights.astype(F32)
            adj_prob = dot(values[window], adjoint, NT)
            shift = sum(
                jnp.sum(wide[part] * adj_prob[part], axis=0, keepdims=True)
                for part in (slice(k, k + HALF) for k in range(0, WINDOW, HALF))
            )
            adj_score = weights * (adj_prob - shift).astype(BF16)
            ds_s[m, t, p] = adj_score
            key_terms.append(dot(adj_score, query) * LN2)
            value_terms.append(dot(weights, adjoint))
        for terms, own, rim in ((key_terms, dk_s, rim_k), (value_terms, dv_s, rim_v)):
            low, high = terms
            rim[pl.ds(0, HALF), lanes] = low[:HALF].astype(BF16)
            rim[pl.ds(HALF, HALF), lanes] = high[2 * HALF :].astype(BF16)
            both = (low[HALF:] + high[: 2 * HALF]).astype(BF16)
            for t in range(tiles):
                own[place(m, t), lanes] = both[t * HALF : (t + 1) * HALF]
        return carry

    def query_back(m, p, carry):
        keys_t = k_s[m, p].T
        lanes = pl.ds(pl.multiple_of(p * LANES, LANES), LANES)
        for t in range(tiles):
            window = slice(t * HALF, t * HALF + WINDOW)
            adj_query = own_head(dot(keys_t[:, window], ds_s[m, t, p])) * HEAD**-0.5
            dq_s[place(m, t), lanes] = adj_query.astype(BF16)
        return carry

    real = lax.broadcasted_iota(jnp.int32, (HALF, LANES), 1) < nvars
    score = sum(back_to_attended(t) for t in range(tiles))
    score = jnp.where(real, score, 0.0)
    loss_acc[0] = jnp.broadcast_to(jnp.sum(score, keepdims=True), (8, LANES))
    loss_start(0)
    rim_copies = [[] for _ in range(count)]
    for m in range(count):
        lax.fori_loop(0, pairs, functools.partial(attend_back, m), 0, unroll=True)
        if m == 1:
            loss_finish(1)
            loss_start(2)

        for c in range(chunks):
            columns = slice(c * COLS, (c + 1) * COLS)
            term = dot(rim_k[...], wk[columns, :], NT) + dot(rim_v[...], wv[columns, :], NT)
            rim_out[m, c] = term.astype(BF16)
            for side, device in enumerate((left, right)):
                copy = remote(
                    rim_out.at[m, c, pl.ds(side * HALF, HALF)],
                    rim_in.at[m, c, pl.ds((1 - side) * HALF, HALF)],
                    rim_send.at[m, c, side],
                    rim_recv.at[m, c, side],
                    {"grid": device},
                )
                copy.start()
                rim_copies[m].append(copy)
        if m == 0:
            loss_finish(0)
            loss_start(1)

    for m in range(count):
        lax.fori_loop(0, pairs, functools.partial(query_back, m), 0, unroll=True)
    def back_own(c, carry):
        columns = pl.ds(pl.multiple_of(c * COLS, COLS), COLS)
        adj_normed[:, columns] = (
            dot(dq_s[...], wq[columns, :], NT)
            + dot(dk_s[...], wk[columns, :], NT)
            + dot(dv_s[...], wv[columns, :], NT)
        )
        adj_mixed[:, columns] = dot(slopes[...], readout[:, columns])
        return carry

    lax.fori_loop(0, chunks, back_own, 0, unroll=True)
    loss_finish(2)
    loss_out[...] = loss_acc[3, 0:1, 0:1] * (1.0 / (realizations * total_points * nvars))

    stores = []
    for m in range(count):
        for copy in rim_copies[m]:
            copy.wait()
        for t in range(tiles):
            part = slice(t * HALF, (t + 1) * HALF)
            mine = place(m, t)
            normed = normed_wide[mine, :]
            inverse = inverse_own[mine, :1]
            rim = jnp.concatenate([rim_in[m, c, part] for c in range(chunks)], axis=1)
            adjoint = adj_normed[mine, :] + rim.astype(F32)
            adjoint = inverse * (
                adjoint
                - jnp.mean(adjoint, axis=-1, keepdims=True)
                - normed * jnp.mean(adjoint * normed, axis=-1, keepdims=True)
            )
            result[m, part] = (adj_mixed[mine, :] + adjoint).astype(BF16)
            rows_out = pl.ds(t * HALF, HALF)
            store = pltpu.make_async_copy(
                result.at[m, rows_out], out.at[m, rows_out], out_sem.at[m, t]
            )
            store.start()
            stores.append(store)
    for store in stores:
        store.wait()


def per_device(
    ens_size,
    grid_size,
    members,
    observed_truth,
    cell_measure,
    reach,
    w_query,
    w_key,
    w_value,
    w_out,
    readout_coefficients,
):
    count, rows, width = members.shape
    nvars = observed_truth.shape[1]
    pairs = width // LANES
    tiles = rows // HALF
    chunks = width // COLS
    all_rows = count * rows
    groups = loss_groups(ens_size, grid_size)
    stages = len(groups)
    most = max(len(numbers) for _, numbers in groups)
    vmem = pl.BlockSpec(memory_space=pltpu.VMEM)
    anywhere = pl.BlockSpec(memory_space=pl.ANY)
    dma = pltpu.SemaphoreType.DMA
    loss, adjoint = pl.pallas_call(
        functools.partial(kernel, ens_size, grid_size, nvars),
        out_shape=(
            jax.ShapeDtypeStruct((1, 1), F32),
            jax.ShapeDtypeStruct(members.shape, BF16),
        ),
        in_specs=[anywhere, vmem, vmem, vmem, anywhere, anywhere, anywhere, anywhere, vmem],
        out_specs=(vmem, anywhere),
        scratch_shapes=[
            pltpu.VMEM((count, rows, width), BF16),
            pltpu.VMEM((count, 2 * HALF, width), BF16),
            pltpu.VMEM((width, width), BF16),
            pltpu.VMEM((width, width), BF16),
            pltpu.VMEM((width, width), BF16),
            pltpu.VMEM((width, width), BF16),
            pltpu.VMEM((LANES, width), BF16),
            pltpu.VMEM((LANES, rows), F32),
            pltpu.VMEM((rows, LANES), F32),
            pltpu.VMEM((rows, LANES), F32),
            pltpu.VMEM((tiles, WINDOW, HALF), F32),
            pltpu.VMEM((all_rows, width), BF16),
            pltpu.VMEM((all_rows, width), F32),
            pltpu.VMEM((all_rows, LANES), F32),
            pltpu.VMEM((2 * HALF, width), BF16),
            pltpu.VMEM((count, pairs, rows, LANES), BF16),
            pltpu.VMEM((count, pairs, rows + 2 * HALF, LANES), BF16),
            pltpu.VMEM((count, pairs, rows + 2 * HALF, LANES), BF16),
            pltpu.VMEM((count, tiles, pairs, WINDOW, 2 * HALF), BF16),
            pltpu.VMEM((count, tiles, pairs, WINDOW, 2 * HALF), BF16),
            pltpu.VMEM((all_rows, width), BF16),
            pltpu.VMEM((tiles, count * HALF, LANES), F32),
            pltpu.VMEM((ens_size, tiles, count, HALF, LANES), BF16),
            pltpu.VMEM((width, LANES), BF16),
            pltpu.VMEM((all_rows, LANES), BF16),
            pltpu.VMEM((all_rows, width), F32),
            pltpu.VMEM((all_rows, width), BF16),
            pltpu.VMEM((all_rows, width), BF16),
            pltpu.VMEM((all_rows, width), BF16),
            pltpu.VMEM((all_rows, width), BF16),
            pltpu.VMEM((2 * HALF, width), BF16),
            pltpu.VMEM((2 * HALF, width), BF16),
            pltpu.VMEM((count, chunks, 2 * HALF, COLS), BF16),
            pltpu.VMEM((count, chunks, 2 * HALF, COLS), BF16),
            pltpu.VMEM((all_rows, width), F32),
            pltpu.VMEM((count, rows, width), BF16),
            pltpu.VMEM((stages + 1, 8, LANES), F32),
            pltpu.VMEM((stages, most, 8, LANES), F32),
            dma((count + 4,)),
            dma((count, tiles)),
            dma((count, 2)),
            dma((count, 2)),
            dma((ens_size - 1, tiles, count)),
            dma((ens_size - 1, tiles, count)),
            dma((count, chunks, 2)),
            dma((count, chunks, 2)),
            dma((stages, most)),
            dma((stages, most)),
        ],
        compiler_params=pltpu.CompilerParams(
            collective_id=0, has_side_effects=True, vmem_limit_bytes=60 * 1024 * 1024
        ),
        cost_estimate=pl.CostEstimate(
            flops=15_000_000_000, bytes_accessed=12_000_000, transcendentals=4_000_000
        ),
    )(
        members,
        observed_truth.T,
        cell_measure.reshape(1, rows),
        reach.reshape(1, rows),
        w_query,
        w_key,
        w_value,
        w_out,
        readout_coefficients.T,
    )
    return loss[0, 0], adjoint


def solution(mesh):
    return jax.shard_map(
        functools.partial(per_device, mesh.shape["ens"], mesh.shape["grid"]),
        mesh=mesh,
        in_specs=(
            P("ens", "grid", None),
            P("grid", None),
            P("grid"),
            P("grid"),
            P(),
            P(),
            P(),
            P(),
            P(),
        ),
        out_specs=(P(), P("ens", "grid", None)),
        check_vma=False,
    )
```

```python
import functools
import math

import jax
import jax.numpy as jnp
from jax import lax
from jax.experimental import pallas as pl
from jax.experimental.pallas import tpu as pltpu
from jax.sharding import PartitionSpec as P

MESH = pl.DeviceIdType.MESH
F32 = jnp.float32
BF16 = jnp.bfloat16
HEAD = 64
HALF = 128
LANES = 128
COLS = 256
WINDOW = 3 * HALF
EPS = 1e-05
SOFT2 = 0.01
SOFT = 0.1
LOG2E = math.log2(math.e)
LN2 = math.log(2.0)

NN = (((1,), (0,)), ((), ()))
NT = (((1,), (1,)), ((), ()))


def dot(a, b, dims=NN):
    return lax.dot_general(a, b, dims, preferred_element_type=F32)


def flip(index, bits):
    turned = index
    for bit in (1 << b for b in range(bits.bit_length())):
        if bits & bit:
            turned = turned + bit * (1 - 2 * ((index // bit) % 2))
    return turned


def tree_sum(terms):
    while len(terms) > 1:
        terms = [terms[n] + terms[n + 1] for n in range(0, len(terms), 2)]
    return terms[0]


def loss_groups(ens_size, grid_size):
    groups = [("ens", tuple(range(1, ens_size)))]
    low = 1
    while low < grid_size:
        high = min(8, grid_size // low)
        groups.append(("grid", tuple(low * n for n in range(1, high))))
        low *= high
    return groups


def normalise(block):
    values = block.astype(F32)
    centred = values - jnp.mean(values, axis=-1, keepdims=True)
    inverse = lax.rsqrt(jnp.mean(centred * centred, axis=-1, keepdims=True) + EPS)
    return centred * inverse, inverse


def per_head(pair):
    low = lax.broadcasted_iota(jnp.int32, pair.shape, 1) < HEAD
    zero = jnp.zeros_like(pair)
    return jnp.concatenate([jnp.where(low, pair, zero), jnp.where(low, zero, pair)], axis=0)


def own_lanes(tall):
    low = lax.broadcasted_iota(jnp.int32, (HALF, LANES), 1) < HEAD
    return jnp.where(low, tall[:HALF], tall[HALF:])


def own_head(wide):
    both = jnp.concatenate([wide[:HEAD, :HALF], wide[HEAD:, HALF:]], axis=0)
    return both.T


def kernel(
    ens_size,
    grid_size,
    nvars,
    members,
    truth_in,
    measure_in,
    reach_in,
    w_query,
    w_key,
    w_value,
    w_out,
    readout_in,
    loss_out,
    out,
    mem,
    halo,
    wq,
    wk,
    wv,
    wo,
    readout,
    truth_t,
    truth,
    measure,
    bias,
    normed_own,
    normed_wide,
    inverse_own,
    normed_halo,
    q_s,
    k_s,
    v_s,
    p_s,
    ds_s,
    attended,
    forecasts,
    shared,
    folded,
    slopes,
    adj_mixed,
    adj_attended,
    dq_s,
    dk_s,
    dv_s,
    rim_k,
    rim_v,
    rim_out,
    rim_in,
    adj_normed,
    result,
    loss_acc,
    loss_in,
    load_sem,
    out_sem,
    halo_send,
    halo_recv,
    ens_send,
    ens_recv,
    rim_send,
    rim_recv,
    loss_send,
    loss_recv,
):
    count, rows, width = members.shape
    pairs = width // LANES
    chunks = width // COLS
    tiles = rows // HALF
    ens = lax.axis_index("ens")
    grid = lax.axis_index("grid")
    right = lax.rem(grid + 1, grid_size)
    left = lax.rem(grid + grid_size - 1, grid_size)
    first = grid * rows
    total_points = rows * grid_size
    ens_partners = [{"ens": flip(ens, n)} for n in range(1, ens_size)]
    position = {"ens": ens, "grid": grid}
    rounds = [
        [{axis: flip(position[axis], n)} for n in numbers]
        for axis, numbers in loss_groups(ens_size, grid_size)
    ]

    def remote(source, target, send, recv, device):
        return pltpu.make_async_remote_copy(
            src_ref=source,
            dst_ref=target,
            send_sem=send,
            recv_sem=recv,
            device_id=device,
            device_id_type=MESH,
        )

    loads = []
    for m in range(count):
        loads.append(pltpu.make_async_copy(members.at[m], mem.at[m], load_sem.at[m]))
    for n, (source, target) in enumerate(((w_query, wq), (w_key, wk), (w_value, wv), (w_out, wo))):
        loads.append(pltpu.make_async_copy(source, target, load_sem.at[count + n]))
    for load in loads:
        load.start()

    barrier = pltpu.get_barrier_semaphore()
    greeted = [{"grid": left}, {"grid": right}] + [device for group in rounds for device in group]
    for device in greeted:
        pl.semaphore_signal(barrier, inc=1, device_id=device, device_id_type=MESH)
    pl.semaphore_wait(barrier, len(greeted))

    halo_copies = []
    for m in range(count):
        to_left = remote(
            members.at[m, pl.ds(0, HALF)],
            halo.at[m, pl.ds(HALF, HALF)],
            halo_send.at[m, 0],
            halo_recv.at[m, 0],
            {"grid": left},
        )
        to_right = remote(
            members.at[m, pl.ds(rows - HALF, HALF)],
            halo.at[m, pl.ds(0, HALF)],
            halo_send.at[m, 1],
            halo_recv.at[m, 1],
            {"grid": right},
        )
        halo_copies.append((to_left, to_right))
    for copy in halo_copies[0]:
        copy.start()

    adj_normed[:LANES, :] = jnp.zeros((LANES, width), F32)
    adj_normed[:nvars, :] = readout_in[...].astype(F32)
    readout[...] = adj_normed[:LANES, :].astype(BF16)
    truth_t[...] = jnp.zeros_like(truth_t)
    truth_t[:nvars, :] = truth_in[...]
    for t in range(tiles):
        part = pl.ds(t * HALF, HALF)
        truth[part, :] = truth_t[:, t * HALF : (t + 1) * HALF].T
        row = jnp.broadcast_to(measure_in[:, t * HALF : (t + 1) * HALF], (HALF, HALF))
        measure[part, :] = row.T
        offset = lax.broadcasted_iota(jnp.int32, (WINDOW, HALF), 0) - HALF
        query = lax.broadcasted_iota(jnp.int32, (WINDOW, HALF), 1)
        point = offset + (first + t * HALF)
        reach = reach_in[:, t * HALF : (t + 1) * HALF]
        inside = (jnp.abs(offset - query) <= reach) & (point >= 0) & (point < total_points)
        bias[t] = jnp.where(inside, 0.0, -1e30).astype(F32)

    def place(m, t):
        return pl.ds((t * count + m) * HALF, HALF)

    for m in range(count):
        loads[m].wait()
        if m:
            for copy in halo_copies[m]:
                copy.start()
        for t in range(tiles):
            normed, inverse = normalise(mem[m, t * HALF : (t + 1) * HALF])
            normed_own[place(m, t), :] = normed.astype(BF16)
            normed_wide[place(m, t), :] = normed
            inverse_own[place(m, t), :] = jnp.broadcast_to(inverse, (HALF, LANES))

    def project_own(weight, target, start, factor, c, carry):
        columns = pl.ds(pl.multiple_of(c * COLS, COLS), COLS)
        result = dot(normed_own[...], weight[:, columns])
        if factor is not None:
            result = result * factor
        result = result.astype(BF16)
        for m in range(count):
            for t in range(tiles):
                first_row = (t * count + m) * HALF
                for j in range(2):
                    target[m, 2 * c + j, pl.ds(start + t * HALF, HALF), :] = result[
                        first_row : first_row + HALF, j * LANES : (j + 1) * LANES
                    ]
        return carry

    loads[count].wait()
    own = ((wq, q_s, 0, HEAD**-0.5 * LOG2E), (wk, k_s, HALF, None), (wv, v_s, HALF, None))
    for n, job in enumerate(own):
        if n:
            loads[count + n].wait()
        lax.fori_loop(0, chunks, functools.partial(project_own, *job), 0, unroll=True)

    def attend(m, some_tiles, p, carry):
        keys = k_s[m, p]
        values = v_s[m, p]
        for t in some_tiles:
            query = per_head(q_s[m, p, t * HALF : (t + 1) * HALF])
            window = slice(t * HALF, t * HALF + WINDOW)
            scores = dot(keys[window], query, NT)
            scores = scores + jnp.concatenate([bias[t]] * 2, axis=1)
            top = jnp.max(scores, axis=0, keepdims=True)
            weights = jnp.exp2(scores - top)
            weights = weights * (1.0 / jnp.sum(weights, axis=0, keepdims=True))
            weights = weights.astype(BF16)
            p_s[m, t, p] = weights
            blended = own_lanes(dot(weights.T, values[window]))
            lanes = pl.ds(pl.multiple_of(p * LANES, LANES), LANES)
            attended[place(m, t), lanes] = blended.astype(BF16)
        return carry

    def attend_all(m, some_tiles):
        lax.fori_loop(0, pairs, functools.partial(attend, m, some_tiles), 0, unroll=True)

    def keys_of_halo(m):
        for copy in halo_copies[m]:
            copy.wait()
        for t in range(2):
            part = pl.ds(t * HALF, HALF)
            normed, _ = normalise(halo[m, part])
            normed_halo[part, :] = normed.astype(BF16)

        def project_halo(c, carry):
            columns = pl.ds(pl.multiple_of(c * COLS, COLS), COLS)
            for weight, target in ((wk, k_s), (wv, v_s)):
                result = dot(normed_halo[...], weight[:, columns]).astype(BF16)
                for j in range(2):
                    lanes = slice(j * LANES, (j + 1) * LANES)
                    target[m, 2 * c + j, pl.ds(0, HALF), :] = result[:HALF, lanes]
                    target[m, 2 * c + j, pl.ds(HALF + rows, HALF), :] = result[HALF:, lanes]
            return carry

        lax.fori_loop(0, chunks, project_halo, 0, unroll=True)

    ens_copies = [[] for _ in range(tiles)]

    def fold_readout(c, carry):
        part = pl.ds(pl.multiple_of(c * COLS, COLS), COLS)
        folded[part, :] = dot(wo[part, :], readout[...], NT).astype(BF16)
        return carry

    def forecast(m, t):
        these = pl.ds(m * HALF, HALF)
        result = forecasts[t, these, :] + dot(attended[place(m, t), :], folded[...])
        forecasts[t, these, :] = result
        shared[0, t, m] = result.astype(BF16)
        for slot in reversed(range(len(ens_partners))):
            copy = remote(
                shared.at[0, t, m],
                shared.at[slot + 1, t, m],
                ens_send.at[slot, t, m],
                ens_recv.at[slot, t, m],
                ens_partners[slot],
            )
            copy.start()
            ens_copies[t].append(copy)

    keys_of_halo(0)
    attend_all(0, range(tiles))
    loads[count + 3].wait()
    lax.fori_loop(0, chunks, fold_readout, 0, unroll=True)
    for m in range(count):
        base = dot(mem[m], readout[...], NT)
        for t in range(tiles):
            forecasts[t, m * HALF : (m + 1) * HALF, :] = base[t * HALF : (t + 1) * HALF]
    for t in range(tiles):
        forecast(0, t)
    for m in range(1, count):
        keys_of_halo(m)
        for t in range(tiles):
            attend_all(m, (t,))
            forecast(m, t)

    realizations = count * ens_size
    factor = 1.0 / (realizations - 1)
    def slopes_of(t):
        part = slice(t * HALF, (t + 1) * HALF)
        weight = measure[part, :]
        score = jnp.zeros((HALF, LANES), F32)
        parts = []
        for m in range(count):
            mine = forecasts[t, m * HALF : (m + 1) * HALF]
            pair_sum = jnp.zeros((HALF, LANES), F32)
            pair_slope = jnp.zeros((HALF, LANES), F32)
            for slot in range(ens_size):
                for other in range(count):
                    theirs = slice(other * HALF, (other + 1) * HALF)
                    if slot == 0 and other == m:
                        continue
                    if slot == 0:
                        gap = mine - forecasts[t, theirs]
                    else:
                        gap = mine - shared[slot, t, other].astype(F32)
                    square = gap * gap + SOFT2
                    root = lax.rsqrt(square)
                    pair_sum = pair_sum + square * root
                    pair_slope = pair_slope + gap * root
            gap = mine - truth[part, :]
            square = gap * gap + SOFT2
            root = lax.rsqrt(square)
            score = score + weight * (square * root - 0.5 * factor * pair_sum)
            parts.append((weight * (gap * root - factor * pair_slope)).astype(BF16))
        return score, jnp.concatenate(parts, axis=0)

    def back_to_attended(t):
        for copy in ens_copies[t]:
            copy.wait()
        score, result = slopes_of(t)
        these = pl.ds(t * count * HALF, count * HALF)
        slopes[these, :] = result

        def back_out(c, carry):
            columns = pl.ds(pl.multiple_of(c * COLS, COLS), COLS)
            adj_attended[these, columns] = dot(result, folded[columns, :], NT).astype(BF16)
            return carry

        lax.fori_loop(0, chunks, back_out, 0, unroll=True)
        return score

    pending = []

    def loss_start(stage):
        copies = []
        for n, device in enumerate(rounds[stage]):
            copy = remote(
                loss_acc.at[stage],
                loss_in.at[stage, n],
                loss_send.at[stage, n],
                loss_recv.at[stage, n],
                device,
            )
            copy.start()
            copies.append(copy)
        pending.append(copies)

    def loss_finish(stage):
        for copy in pending[stage]:
            copy.wait()
        terms = [loss_acc[stage]] + [loss_in[stage, n] for n in range(len(rounds[stage]))]
        loss_acc[stage + 1] = tree_sum(terms)

    def attend_back(m, p, carry):
        keys = k_s[m, p]
        values = v_s[m, p]
        lanes = pl.ds(pl.multiple_of(p * LANES, LANES), LANES)
        key_terms = []
        value_terms = []
        for t in range(tiles):
            window = slice(t * HALF, t * HALF + WINDOW)
            query = per_head(q_s[m, p, t * HALF : (t + 1) * HALF])
            adjoint = per_head(adj_attended[place(m, t), lanes])
            weights = p_s[m, t, p]
            wide = weights.astype(F32)
            adj_prob = dot(values[window], adjoint, NT)
            shift = sum(
                jnp.sum(wide[part] * adj_prob[part], axis=0, keepdims=True)
                for part in (slice(k, k + HALF) for k in range(0, WINDOW, HALF))
            )
            adj_score = weights * (adj_prob - shift).astype(BF16)
            ds_s[m, t, p] = adj_score
            key_terms.append(dot(adj_score, query) * LN2)
            value_terms.append(dot(weights, adjoint))
        for terms, own, rim in ((key_terms, dk_s, rim_k), (value_terms, dv_s, rim_v)):
            low, high = terms
            rim[pl.ds(0, HALF), lanes] = low[:HALF].astype(BF16)
            rim[pl.ds(HALF, HALF), lanes] = high[2 * HALF :].astype(BF16)
            both = (low[HALF:] + high[: 2 * HALF]).astype(BF16)
            for t in range(tiles):
                own[place(m, t), lanes] = both[t * HALF : (t + 1) * HALF]
        return carry

    def query_back(m, p, carry):
        keys_t = k_s[m, p].T
        lanes = pl.ds(pl.multiple_of(p * LANES, LANES), LANES)
        for t in range(tiles):
            window = slice(t * HALF, t * HALF + WINDOW)
            adj_query = own_head(dot(keys_t[:, window], ds_s[m, t, p])) * HEAD**-0.5
            dq_s[place(m, t), lanes] = adj_query.astype(BF16)
        return carry

    real = lax.broadcasted_iota(jnp.int32, (HALF, LANES), 1) < nvars
    score = sum(back_to_attended(t) for t in range(tiles))
    score = jnp.where(real, score, 0.0)
    loss_acc[0] = jnp.broadcast_to(jnp.sum(score, keepdims=True), (8, LANES))
    loss_start(0)
    rim_copies = [[] for _ in range(count)]
    for m in range(count):
        lax.fori_loop(0, pairs, functools.partial(attend_back, m), 0, unroll=True)
        if m == 1:
            loss_finish(1)
            loss_start(2)

        for c in range(chunks):
            columns = slice(c * COLS, (c + 1) * COLS)
            term = dot(rim_k[...], wk[columns, :], NT) + dot(rim_v[...], wv[columns, :], NT)
            rim_out[m, c] = term.astype(BF16)
            for side, device in enumerate((left, right)):
                copy = remote(
                    rim_out.at[m, c, pl.ds(side * HALF, HALF)],
                    rim_in.at[m, c, pl.ds((1 - side) * HALF, HALF)],
                    rim_send.at[m, c, side],
                    rim_recv.at[m, c, side],
                    {"grid": device},
                )
                copy.start()
                rim_copies[m].append(copy)
        if m == 0:
            loss_finish(0)
            loss_start(1)

    for m in range(count):
        lax.fori_loop(0, pairs, functools.partial(query_back, m), 0, unroll=True)
    def back_own(c, carry):
        columns = pl.ds(pl.multiple_of(c * COLS, COLS), COLS)
        adj_normed[:, columns] = (
            dot(dq_s[...], wq[columns, :], NT)
            + dot(dk_s[...], wk[columns, :], NT)
            + dot(dv_s[...], wv[columns, :], NT)
        )
        adj_mixed[:, columns] = dot(slopes[...], readout[:, columns])
        return carry

    lax.fori_loop(0, chunks, back_own, 0, unroll=True)
    loss_finish(2)
    loss_out[...] = loss_acc[3, 0:1, 0:1] * (1.0 / (realizations * total_points * nvars))

    stores = []
    for m in range(count):
        for copy in rim_copies[m]:
            copy.wait()
        for t in range(tiles):
            part = slice(t * HALF, (t + 1) * HALF)
            mine = place(m, t)
            normed = normed_wide[mine, :]
            inverse = inverse_own[mine, :1]
            rim = jnp.concatenate([rim_in[m, c, part] for c in range(chunks)], axis=1)
            adjoint = adj_normed[mine, :] + rim.astype(F32)
            adjoint = inverse * (
                adjoint
                - jnp.mean(adjoint, axis=-1, keepdims=True)
                - normed * jnp.mean(adjoint * normed, axis=-1, keepdims=True)
            )
            result[m, part] = (adj_mixed[mine, :] + adjoint).astype(BF16)
            rows_out = pl.ds(t * HALF, HALF)
            store = pltpu.make_async_copy(
                result.at[m, rows_out], out.at[m, rows_out], out_sem.at[m, t]
            )
            store.start()
            stores.append(store)
    for store in stores:
        store.wait()


def hand_out(source, target, sem):
    count, rows, _ = source.shape
    copies = []
    for m in range(count):
        for t in range(rows // HALF):
            part = pl.ds(t * HALF, HALF)
            copy = pltpu.make_async_copy(source.at[m, part], target.at[m, part], sem.at[m, t])
            copy.start()
            copies.append(copy)
    for copy in copies:
        copy.wait()


def per_device(
    ens_size,
    grid_size,
    members,
    observed_truth,
    cell_measure,
    reach,
    w_query,
    w_key,
    w_value,
    w_out,
    readout_coefficients,
):
    count, rows, width = members.shape
    nvars = observed_truth.shape[1]
    pairs = width // LANES
    tiles = rows // HALF
    chunks = width // COLS
    all_rows = count * rows
    groups = loss_groups(ens_size, grid_size)
    stages = len(groups)
    most = max(len(numbers) for _, numbers in groups)
    vmem = pl.BlockSpec(memory_space=pltpu.VMEM)
    anywhere = pl.BlockSpec(memory_space=pl.ANY)
    dma = pltpu.SemaphoreType.DMA
    loss, adjoint = pl.pallas_call(
        functools.partial(kernel, ens_size, grid_size, nvars),
        out_shape=(
            jax.ShapeDtypeStruct((1, 1), F32),
            jax.ShapeDtypeStruct(members.shape, BF16),
        ),
        in_specs=[anywhere, vmem, vmem, vmem, anywhere, anywhere, anywhere, anywhere, vmem],
        out_specs=(vmem, anywhere),
        scratch_shapes=[
            pltpu.VMEM((count, rows, width), BF16),
            pltpu.VMEM((count, 2 * HALF, width), BF16),
            pltpu.VMEM((width, width), BF16),
            pltpu.VMEM((width, width), BF16),
            pltpu.VMEM((width, width), BF16),
            pltpu.VMEM((width, width), BF16),
            pltpu.VMEM((LANES, width), BF16),
            pltpu.VMEM((LANES, rows), F32),
            pltpu.VMEM((rows, LANES), F32),
            pltpu.VMEM((rows, LANES), F32),
            pltpu.VMEM((tiles, WINDOW, HALF), F32),
            pltpu.VMEM((all_rows, width), BF16),
            pltpu.VMEM((all_rows, width), F32),
            pltpu.VMEM((all_rows, LANES), F32),
            pltpu.VMEM((2 * HALF, width), BF16),
            pltpu.VMEM((count, pairs, rows, LANES), BF16),
            pltpu.VMEM((count, pairs, rows + 2 * HALF, LANES), BF16),
            pltpu.VMEM((count, pairs, rows + 2 * HALF, LANES), BF16),
            pltpu.VMEM((count, tiles, pairs, WINDOW, 2 * HALF), BF16),
            pltpu.VMEM((count, tiles, pairs, WINDOW, 2 * HALF), BF16),
            pltpu.VMEM((all_rows, width), BF16),
            pltpu.VMEM((tiles, count * HALF, LANES), F32),
            pltpu.VMEM((ens_size, tiles, count, HALF, LANES), BF16),
            pltpu.VMEM((width, LANES), BF16),
            pltpu.VMEM((all_rows, LANES), BF16),
            pltpu.VMEM((all_rows, width), F32),
            pltpu.VMEM((all_rows, width), BF16),
            pltpu.VMEM((all_rows, width), BF16),
            pltpu.VMEM((all_rows, width), BF16),
            pltpu.VMEM((all_rows, width), BF16),
            pltpu.VMEM((2 * HALF, width), BF16),
            pltpu.VMEM((2 * HALF, width), BF16),
            pltpu.VMEM((count, chunks, 2 * HALF, COLS), BF16),
            pltpu.VMEM((count, chunks, 2 * HALF, COLS), BF16),
            pltpu.VMEM((all_rows, width), F32),
            pltpu.VMEM((count, rows, width), BF16),
            pltpu.VMEM((stages + 1, 8, LANES), F32),
            pltpu.VMEM((stages, most, 8, LANES), F32),
            dma((count + 4,)),
            dma((count, tiles)),
            dma((count, 2)),
            dma((count, 2)),
            dma((ens_size - 1, tiles, count)),
            dma((ens_size - 1, tiles, count)),
            dma((count, chunks, 2)),
            dma((count, chunks, 2)),
            dma((stages, most)),
            dma((stages, most)),
        ],
        compiler_params=pltpu.CompilerParams(
            collective_id=0, has_side_effects=True, vmem_limit_bytes=60 * 1024 * 1024
        ),
        cost_estimate=pl.CostEstimate(
            flops=15_000_000_000, bytes_accessed=12_000_000, transcendentals=4_000_000
        ),
    )(
        members,
        observed_truth.T,
        cell_measure.reshape(1, rows),
        reach.reshape(1, rows),
        w_query,
        w_key,
        w_value,
        w_out,
        readout_coefficients.T,
    )
    adjoint = pl.pallas_call(
        hand_out,
        out_shape=jax.ShapeDtypeStruct(members.shape, BF16),
        in_specs=[anywhere],
        out_specs=anywhere,
        scratch_shapes=[dma((count, tiles))],
    )(adjoint)
    return loss[0, 0], adjoint


def solution(mesh):
    return jax.shard_map(
        functools.partial(per_device, mesh.shape["ens"], mesh.shape["grid"]),
        mesh=mesh,
        in_specs=(
            P("ens", "grid", None),
            P("grid", None),
            P("grid"),
            P("grid"),
            P(),
            P(),
            P(),
            P(),
            P(),
        ),
        out_specs=(P(), P("ens", "grid", None)),
        check_vma=False,
    )
```
